32 devices in a mesh: vis: 8 (over z, x), head: 4 (over y, core).
Axes of the slice: x: 2, y: 2, z: 4, core: 2. Of those that a mesh axis runs over, the one named last changes fastest.
Arguments:
- patches: bfloat16 [3072, 1280], P('vis'), may hold values from -6 to 6
- norm_gain: float32 [1280], replicated, may hold values from 0.4 to 1.6
- w_qkv: bfloat16 [1280, 3, 1280], P(None, None, 'head'), may hold values from -1 to 1
- w_out: bfloat16 [1280, 1280], P(None, 'head'), may hold values from -0.15625 to 0.15625
- grad_y: bfloat16 [3072, 1280], P('vis'), may hold values from -6 to 6
- window_ids: int32 [3072], replicated, may hold values from 0 to 63, never falling along the last dimension, each value on 1 to 64 neighbouring positions
Outputs:
- grad_x: bfloat16 [3072, 1280], P('vis', 'head')
- grad_qkv: float32 [1280, 3, 1280], P('vis', None, 'head')
- grad_out: float32 [1280, 1280], P('vis', 'head')
- grad_gain: float32 [1280], P('head')
The draws below stay inside these ranges and needn't reach their ends.
Inputs may be any that keep to these rules, and one draw needn't show every extreme that they name: `window_ids`: window numbers never fall along the patches, and each window holds 1 to 64 patches, one exactly 64.
All inputs are finite; a program needn't handle non-finite values.
Results may differ from the reference program's by a relative error of at most 0.03.
Values may be sent and summed in bfloat16 or wider, within the bound.
No kernel may reach another device: no remote copies, remote signals or barrier semaphores. Data moves between devices by JAX's collectives and lax.ppermute only.
A program may use at most 64 MiB of HBM per device.

```python
import math
import jax
import jax.numpy as jnp
import numpy as np
from jax import lax

D = 1280
HEAD_DIM = 80
WIN = 64
ROWS_DEV = 384
ROWS = 3072
WINDOWS = 64


def draw_patches(key, part):
    key = jax.random.fold_in(key, 11)
    noise_key = jax.random.fold_in(key, 0)
    values = jnp.clip(jax.random.normal(noise_key, (ROWS, D), jnp.float32), -6.0, 6.0)
    return values.astype(jnp.bfloat16)


def draw_w_qkv(key, part):
    key = jax.random.fold_in(key, 23)
    base_key = jax.random.fold_in(key, 0)
    values = jnp.clip(jax.random.normal(base_key, (D, 3, D), jnp.float32), -6.0, 6.0) * D ** (-0.5)
    return values.astype(jnp.bfloat16)


def with_spikes(array, own_key, source, target, shards_of, factor):
    def block_of(axis_at):
        return (jnp.arange(array.shape[axis_at]) // (array.shape[axis_at] // shards_of)).reshape((-1,) + (1,) * (array.ndim - 1 - axis_at))

    first = jax.random.permutation(own_key, shards_of)[block_of(target)]
    other_side = (block_of(target) + shards_of // 2) % shards_of
    return jnp.where((block_of(source) == first) | (block_of(source) == other_side), factor * array, array)


def shard_levels(key, dims, shards, low, largest):
    gain = 1.0
    for axis_at, blocks in shards:
        draws = jax.random.uniform(jax.random.fold_in(jax.random.fold_in(key, 6), axis_at), (blocks,), jnp.float32, low / len(shards), largest / len(shards))
        gain = gain * jnp.repeat(jnp.exp(draws), dims[axis_at] // blocks).reshape((-1,) + (1,) * (len(dims) - 1 - axis_at))
    return gain


def length_profile(amount, total, bound, slope):
    weights = [(1 << 20) // math.isqrt(rank ** slope) + 1 for rank in range(2, amount + 1)]
    rest, counts = total - bound - (amount - 1), [1] * (amount - 1)
    while rest > 0:
        free = [i for i in range(amount - 1) if counts[i] < bound]
        mass, budget = sum([weights[i] for i in free]), rest
        for i in free:
            extra = min(bound - counts[i], max(1, budget * weights[i] // mass), rest)
            counts[i] = counts[i] + extra
            rest = rest - extra
    return np.array([bound] + counts)


def uneven(rng, amount, total, bound, skew):
    if amount == 2:
        one = jax.random.randint(rng, (), max(1, total - bound), min(bound, total - 1) + 1)
        return jnp.stack([one, total - one])
    sizes = jnp.asarray(length_profile(amount, total, bound, skew), jnp.int32)
    twos = (amount - 1) // 2
    donor, sink = sizes[1:1 + 2 * twos:2], sizes[2:2 + 2 * twos:2]
    slack = jnp.minimum(donor - 1, bound - sink)
    shifted = jax.random.randint(jax.random.fold_in(rng, 1), (twos,), 0, 1 << 20) % (slack + 1)
    sizes = sizes.at[1:1 + 2 * twos:2].set(donor - shifted).at[2:2 + 2 * twos:2].set(sink + shifted)
    return sizes[jax.random.permutation(jax.random.fold_in(rng, 2), amount)]


def bell_draw(key, shape, deviation, reach, cuts=(), held_as=jnp.bfloat16):
    factor_of = shard_levels(key, shape, cuts, -0.22, 0.18) if cuts else 1.0
    entries = jax.random.normal(key, shape, jnp.float32) * deviation * factor_of
    return jnp.minimum(jnp.maximum(entries, -reach), reach).astype(held_as)


def gaussian_with(rng, dims, width, most, cuts, heavy, kind=jnp.bfloat16):
    values = width * jax.random.normal(rng, dims, jnp.float32)
    if cuts:
        values = values * shard_levels(rng, dims, cuts, -0.22, 0.18)
    return jnp.clip(with_spikes(values, jax.random.fold_in(rng, 3), *heavy), -most, most).astype(kind)


def setup_inputs(seed: int = 0) -> dict:
    seeds = jax.random.split(jax.random.key(seed), 7)
    return {
        "patches": draw_patches(jax.random.fold_in(seeds[6], 71), 0),
        "norm_gain": jnp.clip(1.0 + 0.12 * jax.random.normal(seeds[1], (D,), jnp.float32), 0.4, 1.6),
        "w_qkv": draw_w_qkv(jax.random.fold_in(seeds[6], 71), 0),
        "w_out": bell_draw(seeds[3], (D, D), D ** -0.5, 0.15625, ((1, 4),)),
        "grad_y": gaussian_with(seeds[4], (ROWS, D), 1.0, 6.0, ((0, 8),), (0, 1, 8, 2.0)),
        "window_ids": jnp.searchsorted(jnp.cumsum(uneven(seeds[5], WINDOWS, ROWS, WIN, 0)), jnp.arange(ROWS), side="right").astype(jnp.int32),
    }


norm_epsilon = 1e-06

def attention_grads(query, keyval, own_ids, key_ids, grad_att):
    f32 = jnp.float32
    row_count = query.shape[0]
    key_span = keyval.shape[0]
    heads = query.shape[1] // HEAD_DIM
    scale = HEAD_DIM ** (-0.5)
    q_heads = query.reshape(row_count, heads, HEAD_DIM).astype(f32)
    k_heads = keyval[:, 0].reshape(key_span, heads, HEAD_DIM).astype(f32)
    v_heads = keyval[:, 1].reshape(key_span, heads, HEAD_DIM).astype(f32)
    g_heads = grad_att.reshape(row_count, heads, HEAD_DIM).astype(f32)
    scores = jnp.einsum('rhe,khe->hrk', q_heads, k_heads) * scale
    same_window = own_ids[:, None] == key_ids[None, :]
    scores = jnp.where(same_window[None], scores, -1e+30)
    highest = lax.optimization_barrier(jnp.max(scores, axis=2, keepdims=True))
    weights = jnp.exp(scores - highest)
    weights = weights / lax.optimization_barrier(jnp.sum(weights, axis=2, keepdims=True))
    probs = weights.astype(jnp.bfloat16)
    attended = jnp.einsum('hrk,khe->rhe', probs.astype(f32), v_heads).astype(jnp.bfloat16)
    delta = lax.optimization_barrier(jnp.sum(attended.astype(f32) * g_heads, axis=2))
    dprob = jnp.einsum('rhe,khe->hrk', g_heads, v_heads)
    dscore = (weights * (dprob - jnp.transpose(delta)[:, :, None]) * scale).astype(jnp.bfloat16)
    grad_q = jnp.einsum('hrk,khe->rhe', dscore.astype(f32), k_heads).astype(jnp.bfloat16)
    grad_k = jnp.einsum('hrk,rhe->khe', dscore.astype(f32), q_heads)
    grad_v = jnp.einsum('hrk,rhe->khe', probs.astype(f32), g_heads)
    key_grads = jnp.stack([grad_k.reshape(key_span, -1), grad_v.reshape(key_span, -1)], axis=1)
    return (attended.reshape(row_count, -1), grad_q.reshape(row_count, -1), key_grads)

def reference(patches, norm_gain, w_qkv, w_out, grad_y, window_ids):
    f32 = jnp.float32
    bf16 = jnp.bfloat16
    inputs = patches.astype(f32)
    inverse = lax.rsqrt(lax.optimization_barrier(jnp.mean(inputs * inputs, axis=1, keepdims=True)) + norm_epsilon)
    normed = (inputs * inverse * norm_gain[None, :]).astype(bf16)
    project = jnp.einsum('rd,dcj->rcj', normed.astype(f32), w_qkv.astype(f32)).astype(bf16)
    grad_att = jnp.dot(grad_y, w_out, preferred_element_type=f32).astype(bf16)
    blocks = ROWS // ROWS_DEV
    key_span = ROWS_DEV + 2 * WIN
    padded = jnp.pad(project[:, 1:], ((WIN, WIN), (0, 0), (0, 0)))
    padded_ids = jnp.pad(window_ids, (WIN, WIN), constant_values=-1)
    queries = project[:, 0]

    def one_block(block):
        start = (block * ROWS_DEV).astype(jnp.int32)
        query = lax.dynamic_slice_in_dim(queries, start, ROWS_DEV, 0)
        keyval = lax.dynamic_slice_in_dim(padded, start, key_span, 0)
        own_ids = lax.dynamic_slice_in_dim(window_ids, start, ROWS_DEV, 0)
        key_ids = lax.dynamic_slice_in_dim(padded_ids, start, key_span, 0)
        grad_rows = lax.dynamic_slice_in_dim(grad_att, start, ROWS_DEV, 0)
        return attention_grads(query, keyval, own_ids, key_ids, grad_rows)
    attended, grad_q, key_grads = lax.map(one_block, jnp.arange(blocks, dtype=jnp.int32))
    center = key_grads[:, WIN:WIN + ROWS_DEV]
    upper_rim = key_grads[:, :WIN]
    lower_rim = key_grads[:, WIN + ROWS_DEV:]
    zero_rim = jnp.zeros_like(upper_rim[:1])
    center = center.at[:, ROWS_DEV - WIN:].add(jnp.concatenate([upper_rim[1:], zero_rim], axis=0))
    center = center.at[:, :WIN].add(jnp.concatenate([zero_rim, lower_rim[:-1]], axis=0))
    grad_kv = center.reshape(ROWS, 2, D).astype(bf16)
    attended = attended.reshape(ROWS, D)
    grad_proj = jnp.concatenate([grad_q.reshape(ROWS, 1, D), grad_kv], axis=1)
    grad_normed = jnp.einsum('rcj,dcj->rd', grad_proj.astype(f32), w_qkv.astype(f32))
    grad_qkv = jnp.einsum('rd,rcj->dcj', normed.astype(f32), grad_proj.astype(f32))
    grad_out = jnp.einsum('ro,ri->oi', grad_y.astype(f32), attended.astype(f32))
    grad_gain = lax.optimization_barrier(jnp.sum(grad_normed * inputs * inverse, axis=0))
    scaled = grad_normed * norm_gain[None, :]
    product_mean = lax.optimization_barrier(jnp.mean(scaled * inputs, axis=1, keepdims=True))
    grad_x = (grad_y.astype(f32) + inverse * (scaled - inputs * inverse * inverse * product_mean)).astype(bf16)
    return (grad_x, grad_qkv, grad_out, grad_gain)
```

```python
import functools

import jax
import jax.numpy as jnp
from jax import lax
from jax.experimental import pallas as pl
from jax.experimental.pallas import tpu as pltpu
from jax.sharding import PartitionSpec as P

HEAD_DIM = 80
WIN = 64
TILE = 128
EPSILON = 1e-06
F32 = jnp.float32
BF16 = jnp.bfloat16
VMEM_LIMIT = 24 << 20
WEIGHT = 300

NN = (((1,), (0,)), ((), ()))
NT = (((1,), (1,)), ((), ()))
TN = (((0,), (0,)), ((), ()))


def dot(a, b, dims=NN):
    return lax.dot_general(a, b, dims, preferred_element_type=F32)


ANY = pl.BlockSpec(memory_space=pl.ANY)


def call(kernel, outs, *args, weight=WEIGHT, after=(), own_copies=(), **kwargs):
    size = lambda t: t.size * t.dtype.itemsize
    moved = sum(size(a) for a in args) + sum(size(o) for o in outs)
    whole = pl.BlockSpec(memory_space=pltpu.VMEM)
    hbm = pl.BlockSpec(memory_space=pltpu.HBM)
    specs = [hbm if i in own_copies else whole for i in range(len(args))] + [ANY] * len(after)
    if after:
        body, first = kernel, len(args)
        kernel = lambda *refs: body(*refs[:first], *refs[first + len(after) :])
    args = args + tuple(after)
    return pl.pallas_call(
        kernel,
        in_specs=specs,
        out_shape=outs,
        compiler_params=pltpu.CompilerParams(vmem_limit_bytes=VMEM_LIMIT),
        cost_estimate=pl.CostEstimate(
            flops=weight * 10 * moved, bytes_accessed=weight * moved, transcendentals=0
        ),
        **kwargs,
    )(*args)


def shape(dims, dtype=BF16):
    return jax.ShapeDtypeStruct(dims, dtype)


def turned_row(row, count):
    tile = jnp.transpose(jnp.broadcast_to(row, (TILE, TILE)))
    return jnp.concatenate([tile] * count, axis=1)


def rows_to_columns(ref, out_ref):
    rows, features = ref.shape
    squares = jnp.zeros((8, rows), F32)
    for t in range(features // TILE):
        x = jnp.transpose(ref[:, t * TILE : (t + 1) * TILE])
        out_ref[t * TILE : (t + 1) * TILE, :] = x
        x = x.astype(F32)
        squares = squares + jnp.sum((x * x).reshape(TILE // 8, 8, rows), axis=0)
    return jnp.sum(squares, axis=0, keepdims=True)


def normalise(x_t_ref, inverse, gain_ref, normed_ref, gain_columns=None):
    features, rows = x_t_ref.shape
    for t in range(features // TILE):
        gain = turned_row(gain_ref[t : t + 1, :], rows // TILE)
        normed_ref[span(t), :] = (x_t_ref[span(t), :].astype(F32) * inverse * gain).astype(BF16)
        if gain_columns is not None:
            gain_columns[span(t), :] = gain[:, :TILE]


def span(t):
    return slice(t * TILE, (t + 1) * TILE)


def head_band(h):
    return slice(h * HEAD_DIM, (h + 1) * HEAD_DIM)


def half_shifted(before, after):
    lane = lax.broadcasted_iota(jnp.int32, after.shape, 1)
    return jnp.where(lane < TILE // 2, pltpu.roll(before, TILE // 2, 1), pltpu.roll(after, TILE // 2, 1))


def window_rows(ids_ref, tiles):
    vis, count = lax.axis_index("vis"), lax.axis_size("vis")
    own = tiles - 1
    first = vis * own
    id_row = lambda t: ids_ref[pl.ds(t, 1), :]
    before = jnp.where(vis > 0, id_row(jnp.maximum(first - 1, 0)), -1)
    after = jnp.where(vis < count - 1, id_row(jnp.minimum(first + own, count * own - 1)), -2)
    line = [before] + [id_row(first + t) for t in range(own)] + [after]
    ids = [half_shifted(line[t], line[t + 1]) for t in range(tiles)]
    counts = [row != after[:, :1] for row in ids]
    upper = lax.broadcasted_iota(jnp.int32, (1, TILE), 1) >= TILE // 2
    counts[0] = upper | ((ids[0] == line[1][:, :1]) & (ids[0] >= 0))
    counts[-1] = counts[-1] & ~upper
    return [row.astype(F32) for row in ids], counts


def attention(blocks, heads, ids, q_at, g_at, wide_at, tall_at):
    scale = HEAD_DIM ** (-0.5)
    columns = {t: turned_row(ids[t], 1) for near in blocks.values() for t in near}
    attended, grad_q, grad_k, grad_v = {}, {}, {}, {}
    for b, near in blocks.items():
        bias = [jnp.where(columns[t] == ids[b], 0.0, -1e30) for t in near]
        bias = jnp.concatenate(bias, axis=0)
        wide = lambda c, h: jnp.concatenate([wide_at(c, h, t) for t in near], axis=1)
        tall = lambda c, h: jnp.concatenate([tall_at(c, h, t) for t in near], axis=0)
        q = [q_at(h, b) for h in heads]
        g = [g_at(h, b) for h in heads]
        scores = [dot(tall(0, h), q[h]) for h in heads]
        dprob = [dot(tall(1, h), g[h]) for h in heads]
        weights = []
        for h in heads:
            s = scores[h] * scale + bias
            e = jnp.exp(s - jnp.max(s, axis=0, keepdims=True))
            weights.append(e * (1.0 / jnp.sum(e, axis=0, keepdims=True)))
        probs = [w.astype(BF16) for w in weights]
        attended[b] = [dot(wide(1, h), probs[h]).astype(BF16) for h in heads]
        dscore = []
        for h in heads:
            delta = jnp.sum(attended[b][h].astype(F32) * g[h].astype(F32), axis=0, keepdims=True)
            dscore.append((weights[h] * (dprob[h] - delta) * scale).astype(BF16))
        grad_q[b] = [dot(wide(0, h), dscore[h]).astype(BF16) for h in heads]
        gk = [dot(q[h], dscore[h], NT) for h in heads]
        gv = [dot(g[h], probs[h], NT) for h in heads]
        for i, t in enumerate(near):
            for sums, part in ((grad_k, gk), (grad_v, gv)):
                part = [p[:, span(i)] for p in part]
                sums[t] = [x + y for x, y in zip(sums[t], part)] if t in sums else part
    return attended, grad_q, grad_k, grad_v


def only(rows, value):
    return jnp.where(rows, value, jnp.zeros_like(value))


def own_kernel(
    x_any, gain_any, w_any, gy_any, wo_any, ids_ref,
    normed_ref, gy_t_ref, inverse_ref, x_own_ref, gy_own_ref, gain_own_ref, first_rows_ref,
    kv_ref, attended_ref, gq_ref, gkv_ref, w_ref, wo_ref,
    x_ref, gain_ref, gy_ref, x_t, gain_columns, q_ref, ga_ref, turned, sems,
):
    places, features = x_ref.shape
    share = wo_ref.shape[0]
    tiles = places // TILE
    rows = places - TILE
    own = pl.ds(WIN, rows)
    copies = [
        pltpu.make_async_copy(x_any, x_ref.at[own], sems.at[0]),
        pltpu.make_async_copy(gain_any, gain_ref, sems.at[1]),
        pltpu.make_async_copy(w_any, w_ref, sems.at[2]),
        pltpu.make_async_copy(gy_any, gy_ref.at[own], sems.at[3]),
        pltpu.make_async_copy(wo_any, wo_ref, sems.at[4]),
    ]
    for copy in copies:
        copy.start()
    empty = jnp.zeros((WIN, features), BF16)
    for ref in (x_ref, gy_ref):
        ref[:WIN, :] = empty
        ref[WIN + rows :, :] = empty
    copies[0].wait()
    inverse = lax.rsqrt(rows_to_columns(x_ref, x_t) / features + EPSILON)
    inverse_ref[...] = jnp.broadcast_to(inverse, inverse_ref.shape)
    copies[1].wait()
    normalise(x_t, inverse, gain_ref, normed_ref, gain_columns)
    copies[2].wait()
    q_ref[...] = dot(w_ref[0], normed_ref[...]).astype(BF16)
    for c in range(2):
        kv_ref[c] = dot(w_ref[1 + c], normed_ref[...]).astype(BF16)
    copies[3].wait()
    for t in range(features // TILE):
        gy_t_ref[span(t), :] = jnp.transpose(gy_ref[:, span(t)])
    copies[4].wait()
    ga_ref[...] = dot(wo_ref[...], gy_t_ref[...]).astype(BF16)
    at = pl.ds(pl.multiple_of(lax.axis_index("head") * share, share), share)
    x_own_ref[...] = x_t[at, :]
    gy_own_ref[...] = gy_t_ref[at, :]
    gain_own_ref[...] = gain_columns[at, :]
    first_rows_ref[:WIN, :] = x_ref[WIN : 2 * WIN, :]
    first_rows_ref[WIN:, :] = gy_ref[WIN : 2 * WIN, :]

    heads = range(share // HEAD_DIM)
    for c in range(2):
        for h in heads:
            turned[c, h] = jnp.transpose(kv_ref[c, head_band(h), :])
    ids, counts = window_rows(ids_ref, tiles)
    blocks = {b: [t for t in (b - 1, b, b + 1) if t < tiles] for b in range(1, tiles)}
    attended, grad_q, grad_k, grad_v = attention(
        blocks, heads, ids,
        lambda h, b: q_ref[head_band(h), span(b)], lambda h, b: ga_ref[head_band(h), span(b)],
        lambda c, h, t: kv_ref[c, head_band(h), span(t)], lambda c, h, t: turned[c, h, span(t), :],
    )
    for h in heads:
        for t in range(tiles):
            if t in blocks:
                attended_ref[head_band(h), span(t)] = only(counts[t], attended[t][h])
                gq_ref[head_band(h), span(t)] = only(counts[t], grad_q[t][h])
            gkv_ref[0, head_band(h), span(t)] = only(counts[t], grad_k[t][h])
            gkv_ref[1, head_band(h), span(t)] = only(counts[t], grad_v[t][h])
    attended_ref[:, :TILE] = jnp.zeros((share, TILE), BF16)
    gq_ref[:, :TILE] = jnp.zeros((share, TILE), BF16)


def halo_kernel(
    edge_ref, first_rows_ref, gain_ref, w_ref, wo_ref, ids_ref, kv_ref, attended_in, gq_in, gkv_in,
    inverse_in, x_own_in, gy_own_in,
    attended_ref, gq_ref, gkv_ref, normed_ref, gy_t_ref, inverse_ref, x_own_ref, gy_own_ref,
    both, x_t, near_keys, turned,
):
    features, share = edge_ref.shape[1], wo_ref.shape[0]
    tiles = attended_ref.shape[1] // TILE
    for i in range(2):
        both[i, :WIN, :] = edge_ref[i * WIN : (i + 1) * WIN, :]
        both[i, WIN:, :] = first_rows_ref[i * WIN : (i + 1) * WIN, :]
    inverse = lax.rsqrt(rows_to_columns(both.at[0], x_t) / features + EPSILON)
    normalise(x_t, inverse, gain_ref, normed_ref)
    for t in range(features // TILE):
        gy_t_ref[span(t), :] = jnp.transpose(both[1, :, span(t)])
    q = dot(w_ref[0], normed_ref[...]).astype(BF16)
    g = dot(wo_ref[...], gy_t_ref[...]).astype(BF16)
    heads = range(share // HEAD_DIM)
    for c in range(2):
        near_keys[c, :, :TILE] = dot(w_ref[1 + c], normed_ref[...]).astype(BF16)
        near_keys[c, :, TILE:] = kv_ref[c, :, span(1)]
        for h in heads:
            turned[c, h] = jnp.transpose(near_keys[c, head_band(h), :])
    ids, counts = window_rows(ids_ref, tiles)
    attended, grad_q, grad_k, grad_v = attention(
        {0: [0, 1]}, heads, ids, lambda h, b: q[head_band(h)], lambda h, b: g[head_band(h)],
        lambda c, h, t: near_keys[c, head_band(h), span(t)], lambda c, h, t: turned[c, h, span(t), :],
    )
    rest = slice(TILE, tiles * TILE)
    at = pl.ds(pl.multiple_of(lax.axis_index("head") * share, share), share)
    for out, old, value in (
        (inverse_ref, inverse_in, jnp.broadcast_to(inverse, (8, TILE))),
        (x_own_ref, x_own_in, x_t[at, :]),
        (gy_own_ref, gy_own_in, gy_t_ref[at, :]),
    ):
        out[:, :TILE] = value
        out[:, rest] = old[:, rest]
    attended_ref[:, rest] = attended_in[:, rest]
    gq_ref[:, rest] = gq_in[:, rest]
    for c, sums in ((0, grad_k), (1, grad_v)):
        gkv_ref[c, :, 2 * TILE :] = gkv_in[c, :, 2 * TILE :].astype(BF16)
        for h in heads:
            for t in (0, 1):
                total = gkv_in[c, head_band(h), span(t)] + only(counts[t], sums[t][h])
                gkv_ref[c, head_band(h), span(t)] = total.astype(BF16)
    for h in heads:
        attended_ref[head_band(h), :TILE] = only(counts[0], attended[0][h])
        gq_ref[head_band(h), :TILE] = only(counts[0], grad_q[0][h])


def halo_rows_kernel(x_any, gy_any, out_ref, sems):
    last = pl.ds(x_any.shape[0] - WIN, WIN)
    copies = [
        pltpu.make_async_copy(x_any.at[last], out_ref.at[pl.ds(0, WIN)], sems.at[0]),
        pltpu.make_async_copy(gy_any.at[last], out_ref.at[pl.ds(WIN, WIN)], sems.at[1]),
    ]
    for copy in copies:
        copy.start()
    for copy in copies:
        copy.wait()


def places(left, bit):
    step = 1 << (len(left) - 1 - left.index(bit))
    return [p for p in range(1 << len(left)) if not p & step], step


def side_blocks(left, bit):
    base, step = places(left, bit)
    mine = (lax.axis_index("vis") >> bit) & 1
    return [[p + step * which for p in base] for which in (1 - mine, mine)]


def gathered(own_ref, halo_ref, scratch, part, left, bits):
    sub = part // len(bits)
    to = 0
    for chain, bit in enumerate(bits):
        for side in side_blocks(left, bit):
            for p in side:
                at = pl.ds(pl.multiple_of(p * part + chain * sub, 16), sub)
                scratch[to : to + sub, :TILE] = halo_ref[at, :]
                scratch[to : to + sub, TILE:] = own_ref[at, TILE:]
                to += sub


def out_query_product_kernel(part, left, bits, a_ref, a_halo_ref, b_ref, c_ref, c_halo_ref, d_ref, *refs):
    outs, (a_rows, c_rows) = refs[:-2], refs[-2:]
    share, rows = b_ref.shape
    gathered(a_ref, a_halo_ref, a_rows, part, left, bits)
    gathered(c_ref, c_halo_ref, c_rows, part, left, bits)
    gap = jnp.zeros((-share % TILE, rows), BF16)
    b = jnp.transpose(jnp.concatenate([b_ref[...], gap], axis=0))
    d = jnp.transpose(jnp.concatenate([gap, d_ref[...]], axis=0))
    shared = b.shape[1] - TILE
    count = outs[0].shape[0]
    for i, out in enumerate(outs):
        at = slice(i * count, (i + 1) * count)
        one, two = dot(a_rows[at, :], b), dot(c_rows[at, :], d)
        out[:, :shared] = one[:, :shared].astype(out.dtype)
        out[:, shared : shared + TILE] = (one[:, shared:] + two[:, :TILE]).astype(out.dtype)
        out[:, shared + TILE :] = two[:, TILE:].astype(out.dtype)


def pair_product_kernel(part, left, bits, a_ref, a_halo_ref, b_ref, *refs):
    outs, a_rows = refs[:-1], refs[-1]
    share, rows = b_ref.shape[1:]
    gathered(a_ref, a_halo_ref, a_rows, part, left, bits)
    b = jnp.transpose(b_ref[...].reshape(2 * share, rows))
    count = outs[0].shape[0]
    for i, out in enumerate(outs):
        out[...] = dot(a_rows[i * count : (i + 1) * count, :], b).astype(out.dtype)


def add_kernel(sub, lefts, bits, *refs):
    chains = len(bits)
    ins, outs = refs[: 2 * chains], refs[2 * chains :]
    joined = len(outs) < 2 * chains
    for chain, (left, bit) in enumerate(zip(lefts, bits)):
        keep_ref, came_ref = ins[2 * chain : 2 * chain + 2]
        first = chain if joined else 0
        for side, out in zip(side_blocks(left, bit), outs if joined else outs[2 * chain : 2 * chain + 2]):
            for i, p in enumerate(side):
                at = pl.ds(pl.multiple_of(p * sub, 16), sub)
                total = keep_ref[at, :] + came_ref[at, :].astype(F32)
                out[(first + i) * sub : (first + i + 1) * sub, :] = total.astype(out.dtype)


def split_whole(total, sub, left, bit):
    rows = lambda p: lax.dynamic_slice_in_dim(total, p * sub, sub, 0)
    send, keep = [jnp.concatenate([rows(p) for p in side], axis=0) for side in side_blocks(left, bit)]
    return [send.astype(BF16), keep]


def split_product(product, part, left, bits):
    sub = part // len(bits)
    by_chain = product.reshape(-1, len(bits), sub, product.shape[1])
    out = []
    for chain, bit in enumerate(bits):
        out += split_whole(by_chain[:, chain].reshape(-1, product.shape[1]), sub, left, bit)
    return out


def halves(rows, width, chains):
    return [shape((rows // 2, width)), shape((rows // 2, width), F32)] * chains


def out_query_product(part, left, bits, a, a_halo, b, c, c_halo, d):
    features = a.shape[0]
    share, rows = b.shape
    if part % (16 * len(bits)):
        a = jnp.concatenate([a_halo, a[:, TILE:]], axis=1)
        c = jnp.concatenate([c_halo, c[:, TILE:]], axis=1)
        product = jnp.concatenate([dot(a, b, NT), dot(c, d, NT)], axis=1)
        return split_product(product, part, left, bits)
    return call(
        functools.partial(out_query_product_kernel, part, left, bits),
        halves(features // len(bits), 2 * share, len(bits)), a, a_halo, b, c, c_halo, d,
        scratch_shapes=[pltpu.VMEM((features, rows), BF16)] * 2,
    )


def pair_product(part, left, bits, a, a_halo, b, after):
    features = a.shape[0]
    _, share, rows = b.shape
    if part % (16 * len(bits)):
        a = jnp.concatenate([a_halo, a[:, TILE:]], axis=1)
        return split_product(dot(a, b.reshape(2 * share, rows), NT), part, left, bits)
    return call(
        functools.partial(pair_product_kernel, part, left, bits),
        halves(features // len(bits), 2 * share, len(bits)), a, a_halo, b, after=after,
        scratch_shapes=[pltpu.VMEM((features, rows), BF16)],
    )


def add_split(sub, lefts, bits, pairs, after, weight):
    joined = len(lefts[0]) == 1 and len(set(bits)) == 1
    if sub % 16:
        parts = sum(
            [split_whole(k + c.astype(F32), sub, l, b) for (k, c), l, b in zip(pairs, lefts, bits)], []
        )
        return [jnp.concatenate(parts[i::2], axis=0) for i in range(2)] if joined else parts
    outs = halves(*pairs[0][0].shape, len(bits))
    if joined:
        outs = [shape((len(bits) * sub, o.shape[1]), o.dtype) for o in outs[:2]]
    return call(
        functools.partial(add_kernel, sub, lefts, bits), outs, *[t for pair in pairs for t in pair],
        after=after, weight=weight,
    )


def finish_out_query_kernel(*refs):
    ins, (out_ref, query_ref) = refs[:-2], refs[-2:]
    sub, width = ins[0].shape
    for chain in range(len(ins) // 2):
        total = ins[2 * chain][...] + ins[2 * chain + 1][...].astype(F32)
        rows = slice(chain * sub, (chain + 1) * sub)
        out_ref[rows, :] = total[:, : width // 2]
        query_ref[rows, :] = total[:, width // 2 :]


def finish_kernel(query_ref, *refs):
    ins, qkv_ref = refs[:-1], refs[-1]
    sub, width = ins[0].shape
    qkv_ref[0] = query_ref[...]
    for chain in range(len(ins) // 2):
        total = ins[2 * chain][...] + ins[2 * chain + 1][...].astype(F32)
        rows = slice(chain * sub, (chain + 1) * sub)
        qkv_ref[1, rows, :] = total[:, : width // 2]
        qkv_ref[2, rows, :] = total[:, width // 2 :]


def normed_grad_kernel(gq_ref, gkv_ref, w_ref, gain_ref, x_ref, halo_ref, send_ref, keep_ref):
    half, padded, rows = send_ref.shape
    share = padded - 16
    features = w_ref.shape[2]
    g = [jnp.transpose(gq_ref[...]), jnp.transpose(gkv_ref[0]), jnp.transpose(gkv_ref[1])]
    total = dot(g[0], w_ref[0]) + dot(g[1], w_ref[1]) + dot(g[2], w_ref[2])
    gap = jnp.zeros((TILE - WIN, features), BF16)
    x = jnp.concatenate([halo_ref[:WIN, :], x_ref[...], gap], axis=0)
    sums = jnp.zeros((rows, TILE), F32)
    for t in range(features // TILE):
        sums = sums + total[:, span(t)] * gain_ref[t : t + 1, :] * x[:, span(t)].astype(F32)
    row = jnp.broadcast_to(jnp.sum(jnp.transpose(sums), axis=0, keepdims=True), (16, rows))
    low = row - row.astype(BF16).astype(F32)
    extra = jnp.where(lax.broadcasted_iota(jnp.int32, row.shape, 0) < 8, row, low).astype(BF16)
    turned = jnp.transpose(total.astype(BF16))
    odd = (lax.axis_index("head") & 1) == 1
    for h in range(half):
        even_block = turned[2 * h * share : (2 * h + 1) * share]
        odd_block = turned[(2 * h + 1) * share : (2 * h + 2) * share]
        send_ref[h, :share, :] = jnp.where(odd, even_block, odd_block)
        keep_ref[h, :share, :] = jnp.where(odd, odd_block, even_block)
        send_ref[h, share:, :] = extra
        keep_ref[h, share:, :] = extra


def head_add_kernel(bit, keep_ref, came_ref, send_ref, next_ref):
    mine = (lax.axis_index("head") >> bit) & 1
    for out, which in ((send_ref, 1 - mine), (next_ref, mine)):
        for i in range(out.shape[0]):
            total = keep_ref[2 * i + which].astype(F32) + came_ref[2 * i + which].astype(F32)
            out[i] = total.astype(out.dtype)


def head_finish_kernel(keep_ref, came_ref, gain_ref, inverse_ref, x_ref, gy_ref, gx_ref, halo_ref, gain_out_ref):
    share = gx_ref.shape[0]
    total = keep_ref[0].astype(F32) + came_ref[0].astype(F32)
    mean = (total[share : share + 1] + total[share + 8 : share + 9]) / (share * lax.axis_size("head"))
    x, gy, inverse = x_ref[...].astype(F32), gy_ref[...].astype(F32), inverse_ref[:1, :]
    grad = total[:share]
    scaled = grad * gain_ref[:, :1]
    gx = (gy + inverse * (scaled - x * inverse * inverse * mean)).astype(BF16)
    gx_ref[...] = gx
    halo_ref[...] = gx[:, :TILE]
    column = jnp.sum(grad * x * inverse, axis=1, keepdims=True)
    spread = jnp.broadcast_to(column, (share, TILE))
    spread = jnp.concatenate([spread, jnp.zeros((-share % TILE, TILE), F32)], axis=0)
    gain_out_ref[...] = jnp.transpose(spread)[:8]


def merge_kernel(gx_ref, came_ref, ids_ref, out_ref, token_ref):
    tiles = gx_ref.shape[1] // TILE
    _, counts = window_rows(ids_ref, tiles)
    gx = [gx_ref[:, span(t)].astype(F32) for t in range(tiles)]
    gx[-1] = jnp.where(counts[-1], gx[-1], came_ref[...].astype(F32))
    for t in range(tiles - 1):
        out_ref[:, span(t)] = half_shifted(gx[t], gx[t + 1]).astype(BF16)
    token_ref[...] = jnp.zeros(token_ref.shape, F32)


def gain_add_kernel(own_ref, came_ref, out_ref):
    out_ref[...] = own_ref[...] + came_ref[...]


def swap(block, axis, distance):
    devices = range(lax.axis_size(axis))
    return lax.ppermute(block, axis, [(i, i ^ distance) for i in devices])


def shift(block, axis, by):
    count = lax.axis_size(axis)
    return lax.ppermute(block, axis, [(i, i + by) for i in range(count) if 0 <= i + by < count])


def per_device(patches, norm_gain, w_qkv, w_out, grad_y, window_ids):
    rows, features = patches.shape
    count = lax.axis_size("vis")
    levels = count.bit_length() - 1
    heads_axis = lax.axis_size("head")
    share = features // heads_axis
    part = features // count

    w_t = jnp.transpose(w_qkv, (1, 2, 0))
    wo_t = jnp.transpose(w_out)
    gain = norm_gain.reshape(-1, TILE)
    ids = window_ids.reshape(-1, TILE)
    hbm = lambda t: pltpu.with_memory_space_constraint(t, pltpu.HBM)
    edge_rows = call(
        halo_rows_kernel, [shape((2 * WIN, features))], hbm(patches), hbm(grad_y), weight=1,
        own_copies=(0, 1), scratch_shapes=[pltpu.SemaphoreType.DMA((2,))],
    )
    edge = shift(edge_rows[0], "vis", 1)
    places = rows + TILE
    columns, slim, pair = (features, places), (share, places), (2, share, places)
    (normed, grad_y_t, inverse, x_own, grad_y_own, own_gain, first_rows,
     kv, attended, grad_q, grad_kv, w_here, wo_here) = call(
        own_kernel,
        [shape(columns), shape(columns), shape((8, places), F32), shape(slim), shape(slim),
         shape((share, TILE), F32), shape((2 * WIN, features)),
         shape(pair), shape(slim), shape(slim), shape(pair, F32), shape(w_t.shape), shape(wo_t.shape)],
        hbm(patches), hbm(gain), hbm(w_t), hbm(grad_y), hbm(wo_t), ids,
        weight=1, own_copies=(0, 1, 2, 3, 4),
        scratch_shapes=[
            pltpu.VMEM((places, features), BF16), pltpu.VMEM(gain.shape, F32),
            pltpu.VMEM((places, features), BF16), pltpu.VMEM(columns, BF16),
            pltpu.VMEM((features, TILE), F32), pltpu.VMEM(slim, BF16), pltpu.VMEM(slim, BF16),
            pltpu.VMEM((2, share // HEAD_DIM, places, HEAD_DIM), BF16), pltpu.SemaphoreType.DMA((5,)),
        ],
    )
    (attended, grad_q, grad_kv, normed_halo, grad_y_halo, inverse, x_own, grad_y_own) = call(
        halo_kernel,
        [shape(slim), shape(slim), shape(pair), shape((features, TILE)), shape((features, TILE)),
         shape((8, places), F32), shape(slim), shape(slim)],
        edge, first_rows, gain, w_here, wo_here, ids, kv, attended, grad_q, grad_kv,
        inverse, x_own, grad_y_own,
        weight=1,
        scratch_shapes=[
            pltpu.VMEM((2, TILE, features), BF16), pltpu.VMEM((features, TILE), BF16),
            pltpu.VMEM((2, share, 2 * TILE), BF16),
            pltpu.VMEM((2, share // HEAD_DIM, 2 * TILE, HEAD_DIM), BF16),
        ],
    )

    rest = list(range(3, levels))
    if levels < 3:
        orders_first = orders_second = [list(range(levels))]
    else:
        orders_first = [[1, 0, 2] + rest, [0, 2, 1] + rest]
        orders_second = [[1, 0, 2] + rest, [0, 1, 2] + rest]
    every = list(range(levels - 1, -1, -1))
    sub = part // len(orders_first)
    bits = lambda orders, step: [order[step] for order in orders]

    def exchange(parts, orders, step):
        return [
            (keep, swap(send, "vis", 1 << bit))
            for send, keep, bit in zip(parts[::2], parts[1::2], bits(orders, step))
        ]

    def add(pairs, orders, step, weight, after=()):
        lefts = [[b for b in every if b not in order[:step]] for order in orders]
        return exchange(add_split(sub, lefts, bits(orders, step), pairs, after, weight), orders, step)

    parts = out_query_product(
        part, every, bits(orders_first, 0), grad_y_t, grad_y_halo, attended, normed, normed_halo, grad_q
    )
    first = exchange(parts, orders_first, 0)
    parts = pair_product(
        part, every, bits(orders_second, 0), normed, normed_halo, grad_kv, parts[:1]
    )
    second = exchange(parts, orders_second, 0)

    block = (heads_axis // 2, share + 16, places)
    send, keep = call(
        normed_grad_kernel, [shape(block), shape(block)],
        grad_q, grad_kv, w_here, gain, patches, edge, after=parts[:1],
    )
    tokens = []
    for step in range(1, levels):
        first = add(first, orders_first, step, WEIGHT if step == 1 else 1)
        tokens.append(first[0][:1])
        second = add(second, orders_second, step, WEIGHT, after=tokens[-1])
        tokens.append(second[0][:1])
    tokens = iter([()] + tokens[1:])
    for bit in range(1, heads_axis.bit_length() - 1):
        came = swap(send, "head", 1 << (bit - 1))
        block = (keep.shape[0] // 2,) + keep.shape[1:]
        send, keep = call(
            functools.partial(head_add_kernel, bit), [shape(block), shape(block, F32)], keep, came,
            after=next(tokens, ()),
        )
    came = swap(send, "head", heads_axis // 2)
    grad_x, grad_x_halo, grad_gain = call(
        head_finish_kernel,
        [shape(slim), shape((share, TILE)), shape((8, share + -share % TILE), F32)],
        keep, came, own_gain, inverse, x_own, grad_y_own, after=next(tokens, ()),
    )
    grad_x, token = call(
        merge_kernel, [shape((share, rows)), shape((8, TILE), F32)],
        grad_x, shift(grad_x_halo, "vis", -1), ids, weight=1,
    )
    for i, bit in enumerate(sorted(range(levels), key=lambda bit: (bit != 2, bit))):
        came = swap(grad_gain, "vis", 1 << bit)
        (grad_gain,) = call(
            gain_add_kernel, [shape(grad_gain.shape, F32)], grad_gain, came,
            weight=1, after=(*next(tokens, ()), *((token,) if i == 0 else ())),
        )
    grad_gain = grad_gain[0, :share]
    flat = lambda pairs: [t for pair in pairs for t in pair]
    grad_out, query_part = call(
        finish_out_query_kernel, [shape((part, share), F32)] * 2, *flat(first), weight=10 * WEIGHT
    )
    (grad_qkv,) = call(
        finish_kernel, [shape((3, part, share), F32)], query_part, *flat(second)
    )
    return jnp.transpose(grad_x), jnp.transpose(grad_qkv, (1, 0, 2)), grad_out, grad_gain


def solution(mesh):
    in_specs = (P("vis", None), P(), P(None, None, "head"), P(None, "head"), P("vis", None), P())
    out_specs = (P("vis", "head"), P("vis", None, "head"), P("vis", "head"), P("head"))
    return jax.shard_map(
        per_device, mesh=mesh, in_specs=in_specs, out_specs=out_specs, check_vma=False
    )
```

```python
import functools

import jax
import jax.numpy as jnp
from jax import lax
from jax.experimental import pallas as pl
from jax.experimental.pallas import tpu as pltpu
from jax.sharding import PartitionSpec as P

HEAD_DIM = 80
WIN = 64
TILE = 128
EPSILON = 1e-06
F32 = jnp.float32
BF16 = jnp.bfloat16
VMEM_LIMIT = 24 << 20
WEIGHT = 300

NN = (((1,), (0,)), ((), ()))
NT = (((1,), (1,)), ((), ()))
TN = (((0,), (0,)), ((), ()))


def dot(a, b, dims=NN):
    return lax.dot_general(a, b, dims, preferred_element_type=F32)


ANY = pl.BlockSpec(memory_space=pl.ANY)


def call(kernel, outs, *args, weight=WEIGHT, after=(), own_copies=(), **kwargs):
    size = lambda t: t.size * t.dtype.itemsize
    moved = sum(size(a) for a in args) + sum(size(o) for o in outs)
    whole = pl.BlockSpec(memory_space=pltpu.VMEM)
    hbm = pl.BlockSpec(memory_space=pltpu.HBM)
    specs = [hbm if i in own_copies else whole for i in range(len(args))] + [ANY] * len(after)
    if after:
        body, first = kernel, len(args)
        kernel = lambda *refs: body(*refs[:first], *refs[first + len(after) :])
    args = args + tuple(after)
    return pl.pallas_call(
        kernel,
        in_specs=specs,
        out_shape=outs,
        compiler_params=pltpu.CompilerParams(vmem_limit_bytes=VMEM_LIMIT),
        cost_estimate=pl.CostEstimate(
            flops=weight * 10 * moved, bytes_accessed=weight * moved, transcendentals=0
        ),
        **kwargs,
    )(*args)


def shape(dims, dtype=BF16):
    return jax.ShapeDtypeStruct(dims, dtype)


def turned_row(row, count):
    tile = jnp.transpose(jnp.broadcast_to(row, (TILE, TILE)))
    return jnp.concatenate([tile] * count, axis=1)


def rows_to_columns(ref, out_ref):
    rows, features = ref.shape
    squares = jnp.zeros((8, rows), F32)
    for t in range(features // TILE):
        x = jnp.transpose(ref[:, t * TILE : (t + 1) * TILE])
        out_ref[t * TILE : (t + 1) * TILE, :] = x
        x = x.astype(F32)
        squares = squares + jnp.sum((x * x).reshape(TILE // 8, 8, rows), axis=0)
    return jnp.sum(squares, axis=0, keepdims=True)


def normalise(x_t_ref, inverse, gain_ref, normed_ref, gain_columns=None):
    features, rows = x_t_ref.shape
    for t in range(features // TILE):
        gain = turned_row(gain_ref[t : t + 1, :], rows // TILE)
        normed_ref[span(t), :] = (x_t_ref[span(t), :].astype(F32) * inverse * gain).astype(BF16)
        if gain_columns is not None:
            gain_columns[span(t), :] = gain[:, :TILE]


def span(t):
    return slice(t * TILE, (t + 1) * TILE)


def head_band(h):
    return slice(h * HEAD_DIM, (h + 1) * HEAD_DIM)


def half_shifted(before, after):
    lane = lax.broadcasted_iota(jnp.int32, after.shape, 1)
    return jnp.where(lane < TILE // 2, pltpu.roll(before, TILE // 2, 1), pltpu.roll(after, TILE // 2, 1))


def window_rows(ids_ref, tiles):
    vis, count = lax.axis_index("vis"), lax.axis_size("vis")
    own = tiles - 1
    first = vis * own
    id_row = lambda t: ids_ref[pl.ds(t, 1), :]
    before = jnp.where(vis > 0, id_row(jnp.maximum(first - 1, 0)), -1)
    after = jnp.where(vis < count - 1, id_row(jnp.minimum(first + own, count * own - 1)), -2)
    line = [before] + [id_row(first + t) for t in range(own)] + [after]
    ids = [half_shifted(line[t], line[t + 1]) for t in range(tiles)]
    counts = [row != after[:, :1] for row in ids]
    upper = lax.broadcasted_iota(jnp.int32, (1, TILE), 1) >= TILE // 2
    counts[0] = upper | ((ids[0] == line[1][:, :1]) & (ids[0] >= 0))
    counts[-1] = counts[-1] & ~upper
    return [row.astype(F32) for row in ids], counts


def attention(blocks, heads, ids, q_at, g_at, wide_at, tall_at):
    scale = HEAD_DIM ** (-0.5)
    columns = {t: turned_row(ids[t], 1) for near in blocks.values() for t in near}
    attended, grad_q, grad_k, grad_v = {}, {}, {}, {}
    for b, near in blocks.items():
        bias = [jnp.where(columns[t] == ids[b], 0.0, -1e30) for t in near]
        bias = jnp.concatenate(bias, axis=0)
        wide = lambda c, h: jnp.concatenate([wide_at(c, h, t) for t in near], axis=1)
        tall = lambda c, h: jnp.concatenate([tall_at(c, h, t) for t in near], axis=0)
        q = [q_at(h, b) for h in heads]
        g = [g_at(h, b) for h in heads]
        scores = [dot(tall(0, h), q[h]) for h in heads]
        dprob = [dot(tall(1, h), g[h]) for h in heads]
        weights = []
        for h in heads:
            s = scores[h] * scale + bias
            e = jnp.exp(s - jnp.max(s, axis=0, keepdims=True))
            weights.append(e * (1.0 / jnp.sum(e, axis=0, keepdims=True)))
        probs = [w.astype(BF16) for w in weights]
        attended[b] = [dot(wide(1, h), probs[h]).astype(BF16) for h in heads]
        dscore = []
        for h in heads:
            delta = jnp.sum(attended[b][h].astype(F32) * g[h].astype(F32), axis=0, keepdims=True)
            dscore.append((weights[h] * (dprob[h] - delta) * scale).astype(BF16))
        grad_q[b] = [dot(wide(0, h), dscore[h]).astype(BF16) for h in heads]
        gk = [dot(q[h], dscore[h], NT) for h in heads]
        gv = [dot(g[h], probs[h], NT) for h in heads]
        for i, t in enumerate(near):
            for sums, part in ((grad_k, gk), (grad_v, gv)):
                part = [p[:, span(i)] for p in part]
                sums[t] = [x + y for x, y in zip(sums[t], part)] if t in sums else part
    return attended, grad_q, grad_k, grad_v


def only(rows, value):
    return jnp.where(rows, value, jnp.zeros_like(value))


def own_kernel(
    x_any, gain_any, w_any, gy_any, wo_any, ids_ref,
    normed_ref, gy_t_ref, inverse_ref, x_own_ref, gy_own_ref, gain_own_ref, first_rows_ref,
    kv_ref, attended_ref, gq_ref, gkv_ref, w_ref, wo_ref,
    x_ref, gain_ref, gy_ref, x_t, gain_columns, q_ref, ga_ref, turned, sems,
):
    places, features = x_ref.shape
    share = wo_ref.shape[0]
    tiles = places // TILE
    rows = places - TILE
    own = pl.ds(WIN, rows)
    copies = [
        pltpu.make_async_copy(x_any, x_ref.at[own], sems.at[0]),
        pltpu.make_async_copy(gain_any, gain_ref, sems.at[1]),
        pltpu.make_async_copy(w_any, w_ref, sems.at[2]),
        pltpu.make_async_copy(gy_any, gy_ref.at[own], sems.at[3]),
        pltpu.make_async_copy(wo_any, wo_ref, sems.at[4]),
    ]
    for copy in copies:
        copy.start()
    empty = jnp.zeros((WIN, features), BF16)
    for ref in (x_ref, gy_ref):
        ref[:WIN, :] = empty
        ref[WIN + rows :, :] = empty
    copies[0].wait()
    inverse = lax.rsqrt(rows_to_columns(x_ref, x_t) / features + EPSILON)
    inverse_ref[...] = jnp.broadcast_to(inverse, inverse_ref.shape)
    copies[1].wait()
    normalise(x_t, inverse, gain_ref, normed_ref, gain_columns)
    copies[2].wait()
    q_ref[...] = dot(w_ref[0], normed_ref[...]).astype(BF16)
    for c in range(2):
        kv_ref[c] = dot(w_ref[1 + c], normed_ref[...]).astype(BF16)
    copies[3].wait()
    for t in range(features // TILE):
        gy_t_ref[span(t), :] = jnp.transpose(gy_ref[:, span(t)])
    copies[4].wait()
    ga_ref[...] = dot(wo_ref[...], gy_t_ref[...]).astype(BF16)
    at = pl.ds(pl.multiple_of(lax.axis_index("head") * share, share), share)
    x_own_ref[...] = x_t[at, :]
    gy_own_ref[...] = gy_t_ref[at, :]
    gain_own_ref[...] = gain_columns[at, :]
    first_rows_ref[:WIN, :] = x_ref[WIN : 2 * WIN, :]
    first_rows_ref[WIN:, :] = gy_ref[WIN : 2 * WIN, :]

    heads = range(share // HEAD_DIM)
    for c in range(2):
        for h in heads:
            turned[c, h] = jnp.transpose(kv_ref[c, head_band(h), :])
    ids, counts = window_rows(ids_ref, tiles)
    blocks = {b: [t for t in (b - 1, b, b + 1) if t < tiles] for b in range(1, tiles)}
    attended, grad_q, grad_k, grad_v = attention(
        blocks, heads, ids,
        lambda h, b: q_ref[head_band(h), span(b)], lambda h, b: ga_ref[head_band(h), span(b)],
        lambda c, h, t: kv_ref[c, head_band(h), span(t)], lambda c, h, t: turned[c, h, span(t), :],
    )
    for h in heads:
        for t in range(tiles):
            if t in blocks:
                attended_ref[head_band(h), span(t)] = only(counts[t], attended[t][h])
                gq_ref[head_band(h), span(t)] = only(counts[t], grad_q[t][h])
            gkv_ref[0, head_band(h), span(t)] = only(counts[t], grad_k[t][h])
            gkv_ref[1, head_band(h), span(t)] = only(counts[t], grad_v[t][h])
    attended_ref[:, :TILE] = jnp.zeros((share, TILE), BF16)
    gq_ref[:, :TILE] = jnp.zeros((share, TILE), BF16)


def halo_kernel(
    edge_ref, first_rows_ref, gain_ref, w_ref, wo_ref, ids_ref, kv_ref, attended_in, gq_in, gkv_in,
    inverse_in, x_own_in, gy_own_in,
    attended_ref, gq_ref, gkv_ref, normed_ref, gy_t_ref, inverse_ref, x_own_ref, gy_own_ref,
    both, x_t, near_keys, turned,
):
    features, share = edge_ref.shape[1], wo_ref.shape[0]
    tiles = attended_ref.shape[1] // TILE
    for i in range(2):
        both[i, :WIN, :] = edge_ref[i * WIN : (i + 1) * WIN, :]
        both[i, WIN:, :] = first_rows_ref[i * WIN : (i + 1) * WIN, :]
    inverse = lax.rsqrt(rows_to_columns(both.at[0], x_t) / features + EPSILON)
    normalise(x_t, inverse, gain_ref, normed_ref)
    for t in range(features // TILE):
        gy_t_ref[span(t), :] = jnp.transpose(both[1, :, span(t)])
    q = dot(w_ref[0], normed_ref[...]).astype(BF16)
    g = dot(wo_ref[...], gy_t_ref[...]).astype(BF16)
    heads = range(share // HEAD_DIM)
    for c in range(2):
        near_keys[c, :, :TILE] = dot(w_ref[1 + c], normed_ref[...]).astype(BF16)
        near_keys[c, :, TILE:] = kv_ref[c, :, span(1)]
        for h in heads:
            turned[c, h] = jnp.transpose(near_keys[c, head_band(h), :])
    ids, counts = window_rows(ids_ref, tiles)
    attended, grad_q, grad_k, grad_v = attention(
        {0: [0, 1]}, heads, ids, lambda h, b: q[head_band(h)], lambda h, b: g[head_band(h)],
        lambda c, h, t: near_keys[c, head_band(h), span(t)], lambda c, h, t: turned[c, h, span(t), :],
    )
    rest = slice(TILE, tiles * TILE)
    at = pl.ds(pl.multiple_of(lax.axis_index("head") * share, share), share)
    for out, old, value in (
        (inverse_ref, inverse_in, jnp.broadcast_to(inverse, (8, TILE))),
        (x_own_ref, x_own_in, x_t[at, :]),
        (gy_own_ref, gy_own_in, gy_t_ref[at, :]),
    ):
        out[:, :TILE] = value
        out[:, rest] = old[:, rest]
    attended_ref[:, rest] = attended_in[:, rest]
    gq_ref[:, rest] = gq_in[:, rest]
    for c, sums in ((0, grad_k), (1, grad_v)):
        gkv_ref[c, :, 2 * TILE :] = gkv_in[c, :, 2 * TILE :].astype(BF16)
        for h in heads:
            for t in (0, 1):
                total = gkv_in[c, head_band(h), span(t)] + only(counts[t], sums[t][h])
                gkv_ref[c, head_band(h), span(t)] = total.astype(BF16)
    for h in heads:
        attended_ref[head_band(h), :TILE] = only(counts[0], attended[0][h])
        gq_ref[head_band(h), :TILE] = only(counts[0], grad_q[0][h])


def halo_rows_kernel(x_any, gy_any, out_ref, sems):
    last = pl.ds(x_any.shape[0] - WIN, WIN)
    copies = [
        pltpu.make_async_copy(x_any.at[last], out_ref.at[pl.ds(0, WIN)], sems.at[0]),
        pltpu.make_async_copy(gy_any.at[last], out_ref.at[pl.ds(WIN, WIN)], sems.at[1]),
    ]
    for copy in copies:
        copy.start()
    for copy in copies:
        copy.wait()


def places(left, bit):
    step = 1 << (len(left) - 1 - left.index(bit))
    return [p for p in range(1 << len(left)) if not p & step], step


def side_blocks(left, bit):
    base, step = places(left, bit)
    mine = (lax.axis_index("vis") >> bit) & 1
    return [[p + step * which for p in base] for which in (1 - mine, mine)]


def gathered(own_ref, halo_ref, scratch, part, left, bits, sides=(0, 1)):
    sub = part // len(bits)
    to = 0
    for chain, bit in enumerate(bits):
        blocks = side_blocks(left, bit)
        for side in sides:
            for p in blocks[side]:
                at = pl.ds(pl.multiple_of(p * part + chain * sub, 16), sub)
                scratch[to : to + sub, :TILE] = halo_ref[at, :]
                scratch[to : to + sub, TILE:] = own_ref[at, TILE:]
                to += sub


def out_query_product_kernel(part, left, bits, side, a_ref, a_halo_ref, b_ref, c_ref, c_halo_ref, d_ref, *refs):
    outs, (a_rows, c_rows) = refs[:-2], refs[-2:]
    share, rows = b_ref.shape
    gathered(a_ref, a_halo_ref, a_rows, part, left, bits, (side,))
    gathered(c_ref, c_halo_ref, c_rows, part, left, bits, (side,))
    gap = jnp.zeros((-share % TILE, rows), BF16)
    b = jnp.transpose(jnp.concatenate([b_ref[...], gap], axis=0))
    d = jnp.transpose(jnp.concatenate([gap, d_ref[...]], axis=0))
    shared = b.shape[1] - TILE
    count = outs[0].shape[0]
    for i, out in enumerate(outs):
        at = slice(i * count, (i + 1) * count)
        one, two = dot(a_rows[at, :], b), dot(c_rows[at, :], d)
        out[:, :shared] = one[:, :shared].astype(out.dtype)
        out[:, shared : shared + TILE] = (one[:, shared:] + two[:, :TILE]).astype(out.dtype)
        out[:, shared + TILE :] = two[:, TILE:].astype(out.dtype)


def pair_product_kernel(part, left, bits, a_ref, a_halo_ref, b_ref, *refs):
    outs, a_rows = refs[:-1], refs[-1]
    share, rows = b_ref.shape[1:]
    gathered(a_ref, a_halo_ref, a_rows, part, left, bits)
    b = jnp.transpose(b_ref[...].reshape(2 * share, rows))
    count = outs[0].shape[0]
    for i, out in enumerate(outs):
        out[...] = dot(a_rows[i * count : (i + 1) * count, :], b).astype(out.dtype)


def add_kernel(sub, lefts, bits, *refs):
    chains = len(bits)
    ins, outs = refs[: 2 * chains], refs[2 * chains :]
    joined = len(outs) < 2 * chains
    for chain, (left, bit) in enumerate(zip(lefts, bits)):
        keep_ref, came_ref = ins[2 * chain : 2 * chain + 2]
        first = chain if joined else 0
        for side, out in zip(side_blocks(left, bit), outs if joined else outs[2 * chain : 2 * chain + 2]):
            for i, p in enumerate(side):
                at = pl.ds(pl.multiple_of(p * sub, 16), sub)
                total = keep_ref[at, :] + came_ref[at, :].astype(F32)
                out[(first + i) * sub : (first + i + 1) * sub, :] = total.astype(out.dtype)


def split_whole(total, sub, left, bit):
    rows = lambda p: lax.dynamic_slice_in_dim(total, p * sub, sub, 0)
    send, keep = [jnp.concatenate([rows(p) for p in side], axis=0) for side in side_blocks(left, bit)]
    return [send.astype(BF16), keep]


def split_product(product, part, left, bits):
    sub = part // len(bits)
    by_chain = product.reshape(-1, len(bits), sub, product.shape[1])
    out = []
    for chain, bit in enumerate(bits):
        out += split_whole(by_chain[:, chain].reshape(-1, product.shape[1]), sub, left, bit)
    return out


def halves(rows, width, chains):
    return [shape((rows // 2, width)), shape((rows // 2, width), F32)] * chains


def out_query_product(part, left, bits, a, a_halo, b, c, c_halo, d, side, after=()):
    features = a.shape[0]
    share, rows = b.shape
    if part % (16 * len(bits)):
        a = jnp.concatenate([a_halo, a[:, TILE:]], axis=1)
        c = jnp.concatenate([c_halo, c[:, TILE:]], axis=1)
        product = jnp.concatenate([dot(a, b, NT), dot(c, d, NT)], axis=1)
        return split_product(product, part, left, bits)[side::2]
    return call(
        functools.partial(out_query_product_kernel, part, left, bits, side),
        halves(features // len(bits), 2 * share, len(bits))[side::2],
        a, a_halo, b, c, c_halo, d, after=after, weight=1,
        scratch_shapes=[pltpu.VMEM((features // 2, rows), BF16)] * 2,
    )


def pair_product(part, left, bits, a, a_halo, b, after):
    features = a.shape[0]
    _, share, rows = b.shape
    if part % (16 * len(bits)):
        a = jnp.concatenate([a_halo, a[:, TILE:]], axis=1)
        return split_product(dot(a, b.reshape(2 * share, rows), NT), part, left, bits)
    return call(
        functools.partial(pair_product_kernel, part, left, bits),
        halves(features // len(bits), 2 * share, len(bits)), a, a_halo, b, after=after,
        scratch_shapes=[pltpu.VMEM((features, rows), BF16)],
    )


def add_split(sub, lefts, bits, pairs, after, weight):
    joined = len(lefts[0]) == 1 and len(set(bits)) == 1
    if sub % 16:
        parts = sum(
            [split_whole(k + c.astype(F32), sub, l, b) for (k, c), l, b in zip(pairs, lefts, bits)], []
        )
        return [jnp.concatenate(parts[i::2], axis=0) for i in range(2)] if joined else parts
    outs = halves(*pairs[0][0].shape, len(bits))
    if joined:
        outs = [shape((len(bits) * sub, o.shape[1]), o.dtype) for o in outs[:2]]
    return call(
        functools.partial(add_kernel, sub, lefts, bits), outs, *[t for pair in pairs for t in pair],
        after=after, weight=weight,
    )


def finish_out_query_kernel(*refs):
    ins, (out_ref, query_ref) = refs[:-2], refs[-2:]
    sub, width = ins[0].shape
    for chain in range(len(ins) // 2):
        total = ins[2 * chain][...] + ins[2 * chain + 1][...].astype(F32)
        rows = slice(chain * sub, (chain + 1) * sub)
        out_ref[rows, :] = total[:, : width // 2]
        query_ref[rows, :] = total[:, width // 2 :]


def finish_kernel(query_ref, *refs):
    ins, qkv_ref = refs[:-1], refs[-1]
    sub, width = ins[0].shape
    qkv_ref[0] = query_ref[...]
    for chain in range(len(ins) // 2):
        total = ins[2 * chain][...] + ins[2 * chain + 1][...].astype(F32)
        rows = slice(chain * sub, (chain + 1) * sub)
        qkv_ref[1, rows, :] = total[:, : width // 2]
        qkv_ref[2, rows, :] = total[:, width // 2 :]


def normed_grad_kernel(gq_ref, gkv_ref, w_ref, gain_ref, x_ref, halo_ref, send_ref, keep_ref):
    half, padded, rows = send_ref.shape
    share = padded - 16
    features = w_ref.shape[2]
    g = [jnp.transpose(gq_ref[...]), jnp.transpose(gkv_ref[0]), jnp.transpose(gkv_ref[1])]
    total = dot(g[0], w_ref[0]) + dot(g[1], w_ref[1]) + dot(g[2], w_ref[2])
    gap = jnp.zeros((TILE - WIN, features), BF16)
    x = jnp.concatenate([halo_ref[:WIN, :], x_ref[...], gap], axis=0)
    sums = jnp.zeros((rows, TILE), F32)
    for t in range(features // TILE):
        sums = sums + total[:, span(t)] * gain_ref[t : t + 1, :] * x[:, span(t)].astype(F32)
    row = jnp.broadcast_to(jnp.sum(jnp.transpose(sums), axis=0, keepdims=True), (16, rows))
    low = row - row.astype(BF16).astype(F32)
    extra = jnp.where(lax.broadcasted_iota(jnp.int32, row.shape, 0) < 8, row, low).astype(BF16)
    turned = jnp.transpose(total.astype(BF16))
    odd = (lax.axis_index("head") & 1) == 1
    for h in range(half):
        even_block = turned[2 * h * share : (2 * h + 1) * share]
        odd_block = turned[(2 * h + 1) * share : (2 * h + 2) * share]
        send_ref[h, :share, :] = jnp.where(odd, even_block, odd_block)
        keep_ref[h, :share, :] = jnp.where(odd, odd_block, even_block)
        send_ref[h, share:, :] = extra
        keep_ref[h, share:, :] = extra


def head_add_kernel(bit, keep_ref, came_ref, send_ref, next_ref):
    mine = (lax.axis_index("head") >> bit) & 1
    for out, which in ((send_ref, 1 - mine), (next_ref, mine)):
        for i in range(out.shape[0]):
            total = keep_ref[2 * i + which].astype(F32) + came_ref[2 * i + which].astype(F32)
            out[i] = total.astype(out.dtype)


def head_finish_kernel(keep_ref, came_ref, gain_ref, inverse_ref, x_ref, gy_ref, gx_ref, halo_ref, gain_out_ref):
    share = gx_ref.shape[0]
    total = keep_ref[0].astype(F32) + came_ref[0].astype(F32)
    mean = (total[share : share + 1] + total[share + 8 : share + 9]) / (share * lax.axis_size("head"))
    x, gy, inverse = x_ref[...].astype(F32), gy_ref[...].astype(F32), inverse_ref[:1, :]
    grad = total[:share]
    scaled = grad * gain_ref[:, :1]
    gx = (gy + inverse * (scaled - x * inverse * inverse * mean)).astype(BF16)
    gx_ref[...] = gx
    halo_ref[...] = gx[:, :TILE]
    column = jnp.sum(grad * x * inverse, axis=1, keepdims=True)
    spread = jnp.broadcast_to(column, (share, TILE))
    spread = jnp.concatenate([spread, jnp.zeros((-share % TILE, TILE), F32)], axis=0)
    gain_out_ref[...] = jnp.transpose(spread)[:8]


def merge_kernel(gx_ref, came_ref, ids_ref, out_ref, token_ref):
    tiles = gx_ref.shape[1] // TILE
    _, counts = window_rows(ids_ref, tiles)
    gx = [gx_ref[:, span(t)].astype(F32) for t in range(tiles)]
    gx[-1] = jnp.where(counts[-1], gx[-1], came_ref[...].astype(F32))
    for t in range(tiles - 1):
        out_ref[:, span(t)] = half_shifted(gx[t], gx[t + 1]).astype(BF16)
    token_ref[...] = jnp.zeros(token_ref.shape, F32)


def gain_add_kernel(own_ref, came_ref, out_ref):
    out_ref[...] = own_ref[...] + came_ref[...]


def swap(block, axis, distance):
    devices = range(lax.axis_size(axis))
    return lax.ppermute(block, axis, [(i, i ^ distance) for i in devices])


def shift(block, axis, by):
    count = lax.axis_size(axis)
    return lax.ppermute(block, axis, [(i, i + by) for i in range(count) if 0 <= i + by < count])


def per_device(patches, norm_gain, w_qkv, w_out, grad_y, window_ids):
    rows, features = patches.shape
    count = lax.axis_size("vis")
    levels = count.bit_length() - 1
    heads_axis = lax.axis_size("head")
    share = features // heads_axis
    part = features // count

    w_t = jnp.transpose(w_qkv, (1, 2, 0))
    wo_t = jnp.transpose(w_out)
    gain = norm_gain.reshape(-1, TILE)
    ids = window_ids.reshape(-1, TILE)
    hbm = lambda t: pltpu.with_memory_space_constraint(t, pltpu.HBM)
    edge_rows = call(
        halo_rows_kernel, [shape((2 * WIN, features))], hbm(patches), hbm(grad_y), weight=1,
        own_copies=(0, 1), scratch_shapes=[pltpu.SemaphoreType.DMA((2,))],
    )
    edge = shift(edge_rows[0], "vis", 1)
    places = rows + TILE
    columns, slim, pair = (features, places), (share, places), (2, share, places)
    (normed, grad_y_t, inverse, x_own, grad_y_own, own_gain, first_rows,
     kv, attended, grad_q, grad_kv, w_here, wo_here) = call(
        own_kernel,
        [shape(columns), shape(columns), shape((8, places), F32), shape(slim), shape(slim),
         shape((share, TILE), F32), shape((2 * WIN, features)),
         shape(pair), shape(slim), shape(slim), shape(pair, F32), shape(w_t.shape), shape(wo_t.shape)],
        hbm(patches), hbm(gain), hbm(w_t), hbm(grad_y), hbm(wo_t), ids,
        weight=1, own_copies=(0, 1, 2, 3, 4),
        scratch_shapes=[
            pltpu.VMEM((places, features), BF16), pltpu.VMEM(gain.shape, F32),
            pltpu.VMEM((places, features), BF16), pltpu.VMEM(columns, BF16),
            pltpu.VMEM((features, TILE), F32), pltpu.VMEM(slim, BF16), pltpu.VMEM(slim, BF16),
            pltpu.VMEM((2, share // HEAD_DIM, places, HEAD_DIM), BF16), pltpu.SemaphoreType.DMA((5,)),
        ],
    )
    (attended, grad_q, grad_kv, normed_halo, grad_y_halo, inverse, x_own, grad_y_own) = call(
        halo_kernel,
        [shape(slim), shape(slim), shape(pair), shape((features, TILE)), shape((features, TILE)),
         shape((8, places), F32), shape(slim), shape(slim)],
        edge, first_rows, gain, w_here, wo_here, ids, kv, attended, grad_q, grad_kv,
        inverse, x_own, grad_y_own,
        weight=1,
        scratch_shapes=[
            pltpu.VMEM((2, TILE, features), BF16), pltpu.VMEM((features, TILE), BF16),
            pltpu.VMEM((2, share, 2 * TILE), BF16),
            pltpu.VMEM((2, share // HEAD_DIM, 2 * TILE, HEAD_DIM), BF16),
        ],
    )

    rest = list(range(3, levels))
    if levels < 3:
        orders_first = orders_second = [list(range(levels))]
    else:
        orders_first = [[1, 0, 2] + rest, [0, 2, 1] + rest]
        orders_second = [[1, 0, 2] + rest, [0, 1, 2] + rest]
    every = list(range(levels - 1, -1, -1))
    sub = part // len(orders_first)
    bits = lambda orders, step: [order[step] for order in orders]

    def exchange(parts, orders, step):
        return [
            (keep, swap(send, "vis", 1 << bit))
            for send, keep, bit in zip(parts[::2], parts[1::2], bits(orders, step))
        ]

    def add(pairs, orders, step, weight, after=()):
        lefts = [[b for b in every if b not in order[:step]] for order in orders]
        return exchange(add_split(sub, lefts, bits(orders, step), pairs, after, weight), orders, step)

    first_product = functools.partial(
        out_query_product, part, every, bits(orders_first, 0),
        grad_y_t, grad_y_halo, attended, normed, normed_halo, grad_q,
    )
    sends = first_product(0)
    block = (heads_axis // 2, share + 16, places)
    send, keep = call(
        normed_grad_kernel, [shape(block), shape(block)],
        grad_q, grad_kv, w_here, gain, patches, edge, after=sends[:1],
    )
    parts = pair_product(
        part, every, bits(orders_second, 0), normed, normed_halo, grad_kv, (send,)
    )
    keeps = first_product(1, parts[:1])
    first = exchange([t for pair in zip(sends, keeps) for t in pair], orders_first, 0)
    second = exchange(parts, orders_second, 0)

    tokens = []
    for step in range(1, levels):
        first = add(first, orders_first, step, WEIGHT if step == 1 else 1)
        tokens.append(first[0][:1])
        second = add(second, orders_second, step, WEIGHT, after=tokens[-1])
        tokens.append(second[0][:1])
    tokens = iter([()] + tokens[1:])
    for bit in range(1, heads_axis.bit_length() - 1):
        came = swap(send, "head", 1 << (bit - 1))
        block = (keep.shape[0] // 2,) + keep.shape[1:]
        send, keep = call(
            functools.partial(head_add_kernel, bit), [shape(block), shape(block, F32)], keep, came,
            after=next(tokens, ()),
        )
    came = swap(send, "head", heads_axis // 2)
    grad_x, grad_x_halo, grad_gain = call(
        head_finish_kernel,
        [shape(slim), shape((share, TILE)), shape((8, share + -share % TILE), F32)],
        keep, came, own_gain, inverse, x_own, grad_y_own, after=next(tokens, ()),
    )
    grad_x, token = call(
        merge_kernel, [shape((share, rows)), shape((8, TILE), F32)],
        grad_x, shift(grad_x_halo, "vis", -1), ids, weight=1,
    )
    for i, bit in enumerate(sorted(range(levels), key=lambda bit: (bit != 2, bit))):
        came = swap(grad_gain, "vis", 1 << bit)
        (grad_gain,) = call(
            gain_add_kernel, [shape(grad_gain.shape, F32)], grad_gain, came,
            weight=1, after=(*next(tokens, ()), *((token,) if i == 2 else ())),
        )
    grad_gain = grad_gain[0, :share]
    flat = lambda pairs: [t for pair in pairs for t in pair]
    grad_out, query_part = call(
        finish_out_query_kernel, [shape((part, share), F32)] * 2, *flat(first), weight=10 * WEIGHT
    )
    (grad_qkv,) = call(
        finish_kernel, [shape((3, part, share), F32)], query_part, *flat(second),
        after=(token, grad_gain),
    )
    return jnp.transpose(grad_x), jnp.transpose(grad_qkv, (1, 0, 2)), grad_out, grad_gain


def solution(mesh):
    in_specs = (P("vis", None), P(), P(None, None, "head"), P(None, "head"), P("vis", None), P())
    out_specs = (P("vis", "head"), P("vis", None, "head"), P("vis", "head"), P("head"))
    return jax.shard_map(
        per_device, mesh=mesh, in_specs=in_specs, out_specs=out_specs, check_vma=False
    )
```

```python
import functools

import jax
import jax.numpy as jnp
from jax import lax
from jax.experimental import pallas as pl
from jax.experimental.pallas import tpu as pltpu
from jax.sharding import PartitionSpec as P

HEAD_DIM = 80
WIN = 64
TILE = 128
EPSILON = 1e-06
F32 = jnp.float32
BF16 = jnp.bfloat16
VMEM_LIMIT = 24 << 20
WEIGHT = 300

NN = (((1,), (0,)), ((), ()))
NT = (((1,), (1,)), ((), ()))
TN = (((0,), (0,)), ((), ()))


def dot(a, b, dims=NN):
    return lax.dot_general(a, b, dims, preferred_element_type=F32)


ANY = pl.BlockSpec(memory_space=pl.ANY)


def call(kernel, outs, *args, weight=WEIGHT, after=(), own_copies=(), **kwargs):
    size = lambda t: t.size * t.dtype.itemsize
    moved = sum(size(a) for a in args) + sum(size(o) for o in outs)
    whole = pl.BlockSpec(memory_space=pltpu.VMEM)
    hbm = pl.BlockSpec(memory_space=pltpu.HBM)
    specs = [hbm if i in own_copies else whole for i in range(len(args))] + [ANY] * len(after)
    if after:
        body, first = kernel, len(args)
        kernel = lambda *refs: body(*refs[:first], *refs[first + len(after) :])
    args = args + tuple(after)
    return pl.pallas_call(
        kernel,
        in_specs=specs,
        out_shape=outs,
        compiler_params=pltpu.CompilerParams(vmem_limit_bytes=VMEM_LIMIT),
        cost_estimate=pl.CostEstimate(
            flops=weight * 10 * moved, bytes_accessed=weight * moved, transcendentals=0
        ),
        **kwargs,
    )(*args)


def shape(dims, dtype=BF16):
    return jax.ShapeDtypeStruct(dims, dtype)


def turned_row(row, count):
    tile = jnp.transpose(jnp.broadcast_to(row, (TILE, TILE)))
    return jnp.concatenate([tile] * count, axis=1)


def rows_to_columns(ref, out_ref):
    rows, features = ref.shape
    squares = jnp.zeros((8, rows), F32)
    for t in range(features // TILE):
        x = jnp.transpose(ref[:, t * TILE : (t + 1) * TILE])
        out_ref[t * TILE : (t + 1) * TILE, :] = x
        x = x.astype(F32)
        squares = squares + jnp.sum((x * x).reshape(TILE // 8, 8, rows), axis=0)
    return jnp.sum(squares, axis=0, keepdims=True)


def normalise(x_t_ref, inverse, gain_ref, normed_ref, gain_columns=None):
    features, rows = x_t_ref.shape
    for t in range(features // TILE):
        gain = turned_row(gain_ref[t : t + 1, :], rows // TILE)
        normed_ref[span(t), :] = (x_t_ref[span(t), :].astype(F32) * inverse * gain).astype(BF16)
        if gain_columns is not None:
            gain_columns[span(t), :] = gain[:, :TILE]


def span(t):
    return slice(t * TILE, (t + 1) * TILE)


def head_band(h):
    return slice(h * HEAD_DIM, (h + 1) * HEAD_DIM)


def half_shifted(before, after):
    lane = lax.broadcasted_iota(jnp.int32, after.shape, 1)
    return jnp.where(lane < TILE // 2, pltpu.roll(before, TILE // 2, 1), pltpu.roll(after, TILE // 2, 1))


def window_rows(ids_ref, tiles):
    vis, count = lax.axis_index("vis"), lax.axis_size("vis")
    own = tiles - 1
    first = vis * own
    id_row = lambda t: ids_ref[pl.ds(t, 1), :]
    before = jnp.where(vis > 0, id_row(jnp.maximum(first - 1, 0)), -1)
    after = jnp.where(vis < count - 1, id_row(jnp.minimum(first + own, count * own - 1)), -2)
    line = [before] + [id_row(first + t) for t in range(own)] + [after]
    ids = [half_shifted(line[t], line[t + 1]) for t in range(tiles)]
    counts = [row != after[:, :1] for row in ids]
    upper = lax.broadcasted_iota(jnp.int32, (1, TILE), 1) >= TILE // 2
    counts[0] = upper | ((ids[0] == line[1][:, :1]) & (ids[0] >= 0))
    counts[-1] = counts[-1] & ~upper
    return [row.astype(F32) for row in ids], counts


def attention(blocks, heads, ids, q_at, g_at, wide_at, tall_at):
    scale = HEAD_DIM ** (-0.5)
    columns = {t: turned_row(ids[t], 1) for near in blocks.values() for t in near}
    attended, grad_q, grad_k, grad_v = {}, {}, {}, {}
    for b, near in blocks.items():
        bias = [jnp.where(columns[t] == ids[b], 0.0, -1e30) for t in near]
        bias = jnp.concatenate(bias, axis=0)
        wide = lambda c, h: jnp.concatenate([wide_at(c, h, t) for t in near], axis=1)
        tall = lambda c, h: jnp.concatenate([tall_at(c, h, t) for t in near], axis=0)
        q = [q_at(h, b) for h in heads]
        g = [g_at(h, b) for h in heads]
        scores = [dot(tall(0, h), q[h]) for h in heads]
        dprob = [dot(tall(1, h), g[h]) for h in heads]
        weights = []
        for h in heads:
            s = scores[h] * scale + bias
            e = jnp.exp(s - jnp.max(s, axis=0, keepdims=True))
            weights.append(e * (1.0 / jnp.sum(e, axis=0, keepdims=True)))
        probs = [w.astype(BF16) for w in weights]
        attended[b] = [dot(wide(1, h), probs[h]).astype(BF16) for h in heads]
        dscore = []
        for h in heads:
            delta = jnp.sum(attended[b][h].astype(F32) * g[h].astype(F32), axis=0, keepdims=True)
            dscore.append((weights[h] * (dprob[h] - delta) * scale).astype(BF16))
        grad_q[b] = [dot(wide(0, h), dscore[h]).astype(BF16) for h in heads]
        gk = [dot(q[h], dscore[h], NT) for h in heads]
        gv = [dot(g[h], probs[h], NT) for h in heads]
        for i, t in enumerate(near):
            for sums, part in ((grad_k, gk), (grad_v, gv)):
                part = [p[:, span(i)] for p in part]
                sums[t] = [x + y for x, y in zip(sums[t], part)] if t in sums else part
    return attended, grad_q, grad_k, grad_v


def only(rows, value):
    return jnp.where(rows, value, jnp.zeros_like(value))


def own_kernel(
    x_any, gain_any, w_any, gy_any, wo_any, ids_ref,
    normed_ref, gy_t_ref, inverse_ref, x_own_ref, gy_own_ref, gain_own_ref, first_rows_ref,
    kv_ref, attended_ref, gq_ref, gkv_ref, w_ref, wo_ref,
    x_ref, gain_ref, gy_ref, x_t, gain_columns, q_ref, ga_ref, turned, sems,
):
    places, features = x_ref.shape
    share = wo_ref.shape[0]
    tiles = places // TILE
    rows = places - TILE
    own = pl.ds(WIN, rows)
    copies = [
        pltpu.make_async_copy(x_any, x_ref.at[own], sems.at[0]),
        pltpu.make_async_copy(gain_any, gain_ref, sems.at[1]),
        pltpu.make_async_copy(w_any, w_ref, sems.at[2]),
        pltpu.make_async_copy(gy_any, gy_ref.at[own], sems.at[3]),
        pltpu.make_async_copy(wo_any, wo_ref, sems.at[4]),
    ]
    for copy in copies:
        copy.start()
    empty = jnp.zeros((WIN, features), BF16)
    for ref in (x_ref, gy_ref):
        ref[:WIN, :] = empty
        ref[WIN + rows :, :] = empty
    copies[0].wait()
    inverse = lax.rsqrt(rows_to_columns(x_ref, x_t) / features + EPSILON)
    inverse_ref[...] = jnp.broadcast_to(inverse, inverse_ref.shape)
    copies[1].wait()
    normalise(x_t, inverse, gain_ref, normed_ref, gain_columns)
    copies[2].wait()
    q_ref[...] = dot(w_ref[0], normed_ref[...]).astype(BF16)
    for c in range(2):
        kv_ref[c] = dot(w_ref[1 + c], normed_ref[...]).astype(BF16)
    copies[3].wait()
    for t in range(features // TILE):
        gy_t_ref[span(t), :] = jnp.transpose(gy_ref[:, span(t)])
    copies[4].wait()
    ga_ref[...] = dot(wo_ref[...], gy_t_ref[...]).astype(BF16)
    at = pl.ds(pl.multiple_of(lax.axis_index("head") * share, share), share)
    x_own_ref[...] = x_t[at, :]
    gy_own_ref[...] = gy_t_ref[at, :]
    gain_own_ref[...] = gain_columns[at, :]
    first_rows_ref[:WIN, :] = x_ref[WIN : 2 * WIN, :]
    first_rows_ref[WIN:, :] = gy_ref[WIN : 2 * WIN, :]

    heads = range(share // HEAD_DIM)
    for c in range(2):
        for h in heads:
            turned[c, h] = jnp.transpose(kv_ref[c, head_band(h), :])
    ids, counts = window_rows(ids_ref, tiles)
    blocks = {b: [t for t in (b - 1, b, b + 1) if t < tiles] for b in range(1, tiles)}
    attended, grad_q, grad_k, grad_v = attention(
        blocks, heads, ids,
        lambda h, b: q_ref[head_band(h), span(b)], lambda h, b: ga_ref[head_band(h), span(b)],
        lambda c, h, t: kv_ref[c, head_band(h), span(t)], lambda c, h, t: turned[c, h, span(t), :],
    )
    for h in heads:
        for t in range(tiles):
            if t in blocks:
                attended_ref[head_band(h), span(t)] = only(counts[t], attended[t][h])
                gq_ref[head_band(h), span(t)] = only(counts[t], grad_q[t][h])
            gkv_ref[0, head_band(h), span(t)] = only(counts[t], grad_k[t][h])
            gkv_ref[1, head_band(h), span(t)] = only(counts[t], grad_v[t][h])
    attended_ref[:, :TILE] = jnp.zeros((share, TILE), BF16)
    gq_ref[:, :TILE] = jnp.zeros((share, TILE), BF16)


def halo_kernel(
    edge_ref, first_rows_ref, gain_ref, w_ref, wo_ref, ids_ref, kv_ref, attended_in, gq_in, gkv_in,
    inverse_in, x_own_in, gy_own_in,
    attended_ref, gq_ref, gkv_ref, normed_ref, gy_t_ref, inverse_ref, x_own_ref, gy_own_ref,
    both, x_t, near_keys, turned,
):
    features, share = edge_ref.shape[1], wo_ref.shape[0]
    tiles = attended_ref.shape[1] // TILE
    for i in range(2):
        both[i, :WIN, :] = edge_ref[i * WIN : (i + 1) * WIN, :]
        both[i, WIN:, :] = first_rows_ref[i * WIN : (i + 1) * WIN, :]
    inverse = lax.rsqrt(rows_to_columns(both.at[0], x_t) / features + EPSILON)
    normalise(x_t, inverse, gain_ref, normed_ref)
    for t in range(features // TILE):
        gy_t_ref[span(t), :] = jnp.transpose(both[1, :, span(t)])
    q = dot(w_ref[0], normed_ref[...]).astype(BF16)
    g = dot(wo_ref[...], gy_t_ref[...]).astype(BF16)
    heads = range(share // HEAD_DIM)
    for c in range(2):
        near_keys[c, :, :TILE] = dot(w_ref[1 + c], normed_ref[...]).astype(BF16)
        near_keys[c, :, TILE:] = kv_ref[c, :, span(1)]
        for h in heads:
            turned[c, h] = jnp.transpose(near_keys[c, head_band(h), :])
    ids, counts = window_rows(ids_ref, tiles)
    attended, grad_q, grad_k, grad_v = attention(
        {0: [0, 1]}, heads, ids, lambda h, b: q[head_band(h)], lambda h, b: g[head_band(h)],
        lambda c, h, t: near_keys[c, head_band(h), span(t)], lambda c, h, t: turned[c, h, span(t), :],
    )
    rest = slice(TILE, tiles * TILE)
    at = pl.ds(pl.multiple_of(lax.axis_index("head") * share, share), share)
    for out, old, value in (
        (inverse_ref, inverse_in, jnp.broadcast_to(inverse, (8, TILE))),
        (x_own_ref, x_own_in, x_t[at, :]),
        (gy_own_ref, gy_own_in, gy_t_ref[at, :]),
    ):
        out[:, :TILE] = value
        out[:, rest] = old[:, rest]
    attended_ref[:, rest] = attended_in[:, rest]
    gq_ref[:, rest] = gq_in[:, rest]
    for c, sums in ((0, grad_k), (1, grad_v)):
        gkv_ref[c, :, 2 * TILE :] = gkv_in[c, :, 2 * TILE :].astype(BF16)
        for h in heads:
            for t in (0, 1):
                total = gkv_in[c, head_band(h), span(t)] + only(counts[t], sums[t][h])
                gkv_ref[c, head_band(h), span(t)] = total.astype(BF16)
    for h in heads:
        attended_ref[head_band(h), :TILE] = only(counts[0], attended[0][h])
        gq_ref[head_band(h), :TILE] = only(counts[0], grad_q[0][h])


def halo_rows_kernel(x_any, gy_any, out_ref, sems):
    last = pl.ds(x_any.shape[0] - WIN, WIN)
    copies = [
        pltpu.make_async_copy(x_any.at[last], out_ref.at[pl.ds(0, WIN)], sems.at[0]),
        pltpu.make_async_copy(gy_any.at[last], out_ref.at[pl.ds(WIN, WIN)], sems.at[1]),
    ]
    for copy in copies:
        copy.start()
    for copy in copies:
        copy.wait()


def places(left, bit):
    step = 1 << (len(left) - 1 - left.index(bit))
    return [p for p in range(1 << len(left)) if not p & step], step


def side_blocks(left, bit):
    base, step = places(left, bit)
    mine = (lax.axis_index("vis") >> bit) & 1
    return [[p + step * which for p in base] for which in (1 - mine, mine)]


def gathered(own_ref, halo_ref, scratch, part, left, cuts, sides=(0, 1)):
    to = first = 0
    for rows, bit in cuts:
        blocks = side_blocks(left, bit)
        for side in sides:
            for p in blocks[side]:
                at = pl.ds(pl.multiple_of(p * part + first, 16), rows)
                scratch[to : to + rows, :TILE] = halo_ref[at, :]
                scratch[to : to + rows, TILE:] = own_ref[at, TILE:]
                to += rows
        first += rows


def row_spans(outs):
    at = 0
    for out in outs:
        yield slice(at, at + out.shape[0]), out
        at += out.shape[0]


def out_query_product_kernel(
    part, left, cuts, side, a_ref, a_halo_ref, b_ref, c_ref, c_halo_ref, d_ref, *refs
):
    outs, (a_rows, c_rows) = refs[:-2], refs[-2:]
    share, rows = b_ref.shape
    gathered(a_ref, a_halo_ref, a_rows, part, left, cuts, (side,))
    gathered(c_ref, c_halo_ref, c_rows, part, left, cuts, (side,))
    gap = jnp.zeros((-share % TILE, rows), BF16)
    b = jnp.transpose(jnp.concatenate([b_ref[...], gap], axis=0))
    d = jnp.transpose(jnp.concatenate([gap, d_ref[...]], axis=0))
    shared = b.shape[1] - TILE
    for at, out in row_spans(outs):
        one, two = dot(a_rows[at, :], b), dot(c_rows[at, :], d)
        out[:, :shared] = one[:, :shared].astype(out.dtype)
        out[:, shared : shared + TILE] = (one[:, shared:] + two[:, :TILE]).astype(out.dtype)
        out[:, shared + TILE :] = two[:, TILE:].astype(out.dtype)


def pair_product_kernel(part, left, cuts, a_ref, a_halo_ref, b_ref, *refs):
    outs, a_rows = refs[:-1], refs[-1]
    share, rows = b_ref.shape[1:]
    gathered(a_ref, a_halo_ref, a_rows, part, left, cuts)
    b = jnp.transpose(b_ref[...].reshape(2 * share, rows))
    for at, out in row_spans(outs):
        out[...] = dot(a_rows[at, :], b).astype(out.dtype)


def add_kernel(lefts, cuts, *refs):
    chains = len(cuts)
    ins, outs = refs[: 2 * chains], refs[2 * chains :]
    joined = len(outs) < 2 * chains
    first = 0
    for chain, (left, (rows, bit)) in enumerate(zip(lefts, cuts)):
        keep_ref, came_ref = ins[2 * chain : 2 * chain + 2]
        for side, out in zip(side_blocks(left, bit), outs if joined else outs[2 * chain : 2 * chain + 2]):
            for i, p in enumerate(side):
                at = pl.ds(pl.multiple_of(p * rows, 16), rows)
                total = keep_ref[at, :] + came_ref[at, :].astype(F32)
                to = first + i * rows
                out[to : to + rows, :] = total.astype(out.dtype)
        first += rows if joined else 0


def split_whole(total, rows, left, bit):
    block = lambda p: lax.dynamic_slice_in_dim(total, p * rows, rows, 0)
    send, keep = [jnp.concatenate([block(p) for p in side], axis=0) for side in side_blocks(left, bit)]
    return [send.astype(BF16), keep]


def split_product(product, part, left, cuts):
    blocks = product.reshape(-1, part, product.shape[1])
    out = []
    first = 0
    for rows, bit in cuts:
        mine = blocks[:, first : first + rows].reshape(-1, product.shape[1])
        out += split_whole(mine, rows, left, bit)
        first += rows
    return out


def whole_tiles(cuts):
    return all(rows % 16 == 0 for rows, _ in cuts)


def halves(blocks, width, cuts):
    out = []
    for rows, _ in cuts:
        out += [shape((blocks // 2 * rows, width)), shape((blocks // 2 * rows, width), F32)]
    return out


def out_query_product(part, left, cuts, a, a_halo, b, c, c_halo, d, side, after=()):
    features = a.shape[0]
    share, rows = b.shape
    if not whole_tiles(cuts):
        a = jnp.concatenate([a_halo, a[:, TILE:]], axis=1)
        c = jnp.concatenate([c_halo, c[:, TILE:]], axis=1)
        product = jnp.concatenate([dot(a, b, NT), dot(c, d, NT)], axis=1)
        return split_product(product, part, left, cuts)[side::2]
    return call(
        functools.partial(out_query_product_kernel, part, left, cuts, side),
        halves(features // part, 2 * share, cuts)[side::2],
        a, a_halo, b, c, c_halo, d, after=after, weight=1,
        scratch_shapes=[pltpu.VMEM((features // 2, rows), BF16)] * 2,
    )


def pair_product(part, left, cuts, a, a_halo, b, after):
    features = a.shape[0]
    _, share, rows = b.shape
    if not whole_tiles(cuts):
        a = jnp.concatenate([a_halo, a[:, TILE:]], axis=1)
        return split_product(dot(a, b.reshape(2 * share, rows), NT), part, left, cuts)
    return call(
        functools.partial(pair_product_kernel, part, left, cuts),
        halves(features // part, 2 * share, cuts), a, a_halo, b, after=after,
        scratch_shapes=[pltpu.VMEM((features, rows), BF16)],
    )


def add_split(lefts, cuts, pairs, after, weight):
    joined = len(lefts[0]) == 1 and len({bit for _, bit in cuts}) == 1
    if not whole_tiles(cuts):
        parts = []
        for (keep, came), left, (rows, bit) in zip(pairs, lefts, cuts):
            parts += split_whole(keep + came.astype(F32), rows, left, bit)
        return [jnp.concatenate(parts[i::2], axis=0) for i in range(2)] if joined else parts
    width = pairs[0][0].shape[1]
    outs = halves(1 << len(lefts[0]), width, cuts)
    if joined:
        rows = sum(rows for rows, _ in cuts)
        outs = [shape((rows, width)), shape((rows, width), F32)]
    return call(
        functools.partial(add_kernel, lefts, cuts), outs, *[t for pair in pairs for t in pair],
        after=after, weight=weight,
    )


def summed(ins):
    at = 0
    for keep, came in zip(ins[::2], ins[1::2]):
        rows = keep.shape[0]
        yield slice(at, at + rows), keep[...] + came[...].astype(F32)
        at += rows


def finish_out_query_kernel(*refs):
    ins, (out_ref, query_ref) = refs[:-2], refs[-2:]
    share = out_ref.shape[1]
    for rows, total in summed(ins):
        out_ref[rows, :] = total[:, :share]
        query_ref[rows, :] = total[:, share:]


def finish_kernel(query_ref, *refs):
    ins, qkv_ref = refs[:-1], refs[-1]
    share = qkv_ref.shape[2]
    qkv_ref[0] = query_ref[...]
    for rows, total in summed(ins):
        qkv_ref[1, rows, :] = total[:, :share]
        qkv_ref[2, rows, :] = total[:, share:]


def normed_grad_kernel(gq_ref, gkv_ref, w_ref, gain_ref, x_ref, halo_ref, send_ref, keep_ref):
    half, padded, rows = send_ref.shape
    share = padded - 16
    features = w_ref.shape[2]
    g = [jnp.transpose(gq_ref[...]), jnp.transpose(gkv_ref[0]), jnp.transpose(gkv_ref[1])]
    total = dot(g[0], w_ref[0]) + dot(g[1], w_ref[1]) + dot(g[2], w_ref[2])
    gap = jnp.zeros((TILE - WIN, features), BF16)
    x = jnp.concatenate([halo_ref[:WIN, :], x_ref[...], gap], axis=0)
    sums = jnp.zeros((rows, TILE), F32)
    for t in range(features // TILE):
        sums = sums + total[:, span(t)] * gain_ref[t : t + 1, :] * x[:, span(t)].astype(F32)
    row = jnp.broadcast_to(jnp.sum(jnp.transpose(sums), axis=0, keepdims=True), (16, rows))
    low = row - row.astype(BF16).astype(F32)
    extra = jnp.where(lax.broadcasted_iota(jnp.int32, row.shape, 0) < 8, row, low).astype(BF16)
    turned = jnp.transpose(total.astype(BF16))
    odd = (lax.axis_index("head") & 1) == 1
    for h in range(half):
        even_block = turned[2 * h * share : (2 * h + 1) * share]
        odd_block = turned[(2 * h + 1) * share : (2 * h + 2) * share]
        send_ref[h, :share, :] = jnp.where(odd, even_block, odd_block)
        keep_ref[h, :share, :] = jnp.where(odd, odd_block, even_block)
        send_ref[h, share:, :] = extra
        keep_ref[h, share:, :] = extra


def head_add_kernel(bit, keep_ref, came_ref, send_ref, next_ref):
    mine = (lax.axis_index("head") >> bit) & 1
    for out, which in ((send_ref, 1 - mine), (next_ref, mine)):
        for i in range(out.shape[0]):
            total = keep_ref[2 * i + which].astype(F32) + came_ref[2 * i + which].astype(F32)
            out[i] = total.astype(out.dtype)


def head_finish_kernel(keep_ref, came_ref, gain_ref, inverse_ref, x_ref, gy_ref, gx_ref, halo_ref, gain_out_ref):
    share = gx_ref.shape[0]
    total = keep_ref[0].astype(F32) + came_ref[0].astype(F32)
    mean = (total[share : share + 1] + total[share + 8 : share + 9]) / (share * lax.axis_size("head"))
    x, gy, inverse = x_ref[...].astype(F32), gy_ref[...].astype(F32), inverse_ref[:1, :]
    grad = total[:share]
    scaled = grad * gain_ref[:, :1]
    gx = (gy + inverse * (scaled - x * inverse * inverse * mean)).astype(BF16)
    gx_ref[...] = gx
    halo_ref[...] = gx[:, :TILE]
    column = jnp.sum(grad * x * inverse, axis=1, keepdims=True)
    spread = jnp.broadcast_to(column, (share, TILE))
    spread = jnp.concatenate([spread, jnp.zeros((-share % TILE, TILE), F32)], axis=0)
    gain_out_ref[...] = jnp.transpose(spread)[:8]


def merge_kernel(gx_ref, came_ref, ids_ref, out_ref, token_ref):
    tiles = gx_ref.shape[1] // TILE
    _, counts = window_rows(ids_ref, tiles)
    gx = [gx_ref[:, span(t)].astype(F32) for t in range(tiles)]
    gx[-1] = jnp.where(counts[-1], gx[-1], came_ref[...].astype(F32))
    for t in range(tiles - 1):
        out_ref[:, span(t)] = half_shifted(gx[t], gx[t + 1]).astype(BF16)
    token_ref[...] = jnp.zeros(token_ref.shape, F32)


def gain_add_kernel(own_ref, came_ref, out_ref):
    out_ref[...] = own_ref[...] + came_ref[...]


def swap(block, axis, distance):
    devices = range(lax.axis_size(axis))
    return lax.ppermute(block, axis, [(i, i ^ distance) for i in devices])


def shift(block, axis, by):
    count = lax.axis_size(axis)
    return lax.ppermute(block, axis, [(i, i + by) for i in range(count) if 0 <= i + by < count])


def per_device(patches, norm_gain, w_qkv, w_out, grad_y, window_ids):
    rows, features = patches.shape
    count = lax.axis_size("vis")
    levels = count.bit_length() - 1
    heads_axis = lax.axis_size("head")
    share = features // heads_axis
    part = features // count

    w_t = jnp.transpose(w_qkv, (1, 2, 0))
    wo_t = jnp.transpose(w_out)
    gain = norm_gain.reshape(-1, TILE)
    ids = window_ids.reshape(-1, TILE)
    hbm = lambda t: pltpu.with_memory_space_constraint(t, pltpu.HBM)
    edge_rows = call(
        halo_rows_kernel, [shape((2 * WIN, features))], hbm(patches), hbm(grad_y), weight=1,
        own_copies=(0, 1), scratch_shapes=[pltpu.SemaphoreType.DMA((2,))],
    )
    edge = shift(edge_rows[0], "vis", 1)
    places = rows + TILE
    columns, slim, pair = (features, places), (share, places), (2, share, places)
    (normed, grad_y_t, inverse, x_own, grad_y_own, own_gain, first_rows,
     kv, attended, grad_q, grad_kv, w_here, wo_here) = call(
        own_kernel,
        [shape(columns), shape(columns), shape((8, places), F32), shape(slim), shape(slim),
         shape((share, TILE), F32), shape((2 * WIN, features)),
         shape(pair), shape(slim), shape(slim), shape(pair, F32), shape(w_t.shape), shape(wo_t.shape)],
        hbm(patches), hbm(gain), hbm(w_t), hbm(grad_y), hbm(wo_t), ids,
        weight=1, own_copies=(0, 1, 2, 3, 4),
        scratch_shapes=[
            pltpu.VMEM((places, features), BF16), pltpu.VMEM(gain.shape, F32),
            pltpu.VMEM((places, features), BF16), pltpu.VMEM(columns, BF16),
            pltpu.VMEM((features, TILE), F32), pltpu.VMEM(slim, BF16), pltpu.VMEM(slim, BF16),
            pltpu.VMEM((2, share // HEAD_DIM, places, HEAD_DIM), BF16), pltpu.SemaphoreType.DMA((5,)),
        ],
    )
    (attended, grad_q, grad_kv, normed_halo, grad_y_halo, inverse, x_own, grad_y_own) = call(
        halo_kernel,
        [shape(slim), shape(slim), shape(pair), shape((features, TILE)), shape((features, TILE)),
         shape((8, places), F32), shape(slim), shape(slim)],
        edge, first_rows, gain, w_here, wo_here, ids, kv, attended, grad_q, grad_kv,
        inverse, x_own, grad_y_own,
        weight=1,
        scratch_shapes=[
            pltpu.VMEM((2, TILE, features), BF16), pltpu.VMEM((features, TILE), BF16),
            pltpu.VMEM((2, share, 2 * TILE), BF16),
            pltpu.VMEM((2, share // HEAD_DIM, 2 * TILE, HEAD_DIM), BF16),
        ],
    )

    rest = list(range(3, levels))
    if levels < 3:
        orders_first = orders_second = [list(range(levels))]
    else:
        orders_first = [[1, 0, 2] + rest, [0, 2, 1] + rest]
        orders_second = [[1, 0, 2] + rest, [0, 1, 2] + rest]
    every = list(range(levels - 1, -1, -1))
    def sizes(orders):
        if len(orders) == 1:
            return [part]
        short = part // 2 if part % 32 or orders is orders_first else part * 2 // 5 // 16 * 16
        return [short, part - short]

    cuts = lambda orders, step: [(rows, order[step]) for rows, order in zip(sizes(orders), orders)]

    def exchange(parts, orders, step):
        return [
            (keep, swap(send, "vis", 1 << bit))
            for send, keep, (_, bit) in zip(parts[::2], parts[1::2], cuts(orders, step))
        ]

    def add(pairs, orders, step, weight, after=()):
        lefts = [[b for b in every if b not in order[:step]] for order in orders]
        return exchange(add_split(lefts, cuts(orders, step), pairs, after, weight), orders, step)

    first_product = functools.partial(
        out_query_product, part, every, cuts(orders_first, 0),
        grad_y_t, grad_y_halo, attended, normed, normed_halo, grad_q,
    )
    sends = first_product(0)
    block = (heads_axis // 2, share + 16, places)
    send, keep = call(
        normed_grad_kernel, [shape(block), shape(block)],
        grad_q, grad_kv, w_here, gain, patches, edge, after=sends[:1],
    )
    parts = pair_product(
        part, every, cuts(orders_second, 0), normed, normed_halo, grad_kv, (send,)
    )
    keeps = first_product(1, parts[:1])
    first = exchange([t for pair in zip(sends, keeps) for t in pair], orders_first, 0)
    second = exchange(parts, orders_second, 0)

    tokens = []
    for step in range(1, levels):
        first = add(first, orders_first, step, WEIGHT if step == 1 else 1)
        tokens.append(first[0][:1])
        second = add(second, orders_second, step, WEIGHT, after=tokens[-1])
        tokens.append(second[0][:1])
    tokens = iter([()] + tokens[1:])
    for bit in range(1, heads_axis.bit_length() - 1):
        came = swap(send, "head", 1 << (bit - 1))
        block = (keep.shape[0] // 2,) + keep.shape[1:]
        send, keep = call(
            functools.partial(head_add_kernel, bit), [shape(block), shape(block, F32)], keep, came,
            after=next(tokens, ()),
        )
    came = swap(send, "head", heads_axis // 2)
    grad_x, grad_x_halo, grad_gain = call(
        head_finish_kernel,
        [shape(slim), shape((share, TILE)), shape((8, share + -share % TILE), F32)],
        keep, came, own_gain, inverse, x_own, grad_y_own, after=next(tokens, ()),
    )
    grad_x, token = call(
        merge_kernel, [shape((share, rows)), shape((8, TILE), F32)],
        grad_x, shift(grad_x_halo, "vis", -1), ids, weight=1,
    )
    for bit in range(levels):
        came = swap(grad_gain, "vis", 1 << bit)
        (grad_gain,) = call(
            gain_add_kernel, [shape(grad_gain.shape, F32)], grad_gain, came,
            weight=1, after=(*next(tokens, ()), *((token,) if bit == 2 else ())),
        )
    grad_gain = grad_gain[0, :share]
    flat = lambda pairs: [t for pair in pairs for t in pair]
    grad_out, query_part = call(
        finish_out_query_kernel, [shape((part, share), F32)] * 2, *flat(first), weight=10 * WEIGHT
    )
    (grad_qkv,) = call(
        finish_kernel, [shape((3, part, share), F32)], query_part, *flat(second),
        after=(token, grad_gain),
    )
    return jnp.transpose(grad_x), jnp.transpose(grad_qkv, (1, 0, 2)), grad_out, grad_gain


def solution(mesh):
    in_specs = (P("vis", None), P(), P(None, None, "head"), P(None, "head"), P("vis", None), P())
    out_specs = (P("vis", "head"), P("vis", None, "head"), P("vis", "head"), P("head"))
    return jax.shard_map(
        per_device, mesh=mesh, in_specs=in_specs, out_specs=out_specs, check_vma=False
    )
```
